32 devices in a mesh: seq: 8 (over z, y), head: 4 (over x, core).
Axes of the slice: x: 2, y: 2, z: 4, core: 2. Of those that a mesh axis runs over, the one named last changes fastest.
Arguments:
- queries: bfloat16 [4096, 6144], P('seq', 'head'), may hold values from -6 to 6
- keys: bfloat16 [4096, 6144], P('seq', 'head'), may hold values from -6 to 6
- values: bfloat16 [4096, 6144], P('seq', 'head'), may hold values from -6 to 6
- attn_out: bfloat16 [4096, 6144], P('seq', 'head'), may hold values from -120 to 120
- out_grad: bfloat16 [4096, 6144], P('seq', 'head'), may hold values from -6 to 6
- norm_gain: float32 [6144], P('head'), may hold values from 0.5 to 2
Outputs:
- query_grad: bfloat16 [4096, 6144], P('seq', 'head')
- key_grad: bfloat16 [4096, 6144], P('seq', 'head')
- value_grad: bfloat16 [4096, 6144], P('seq', 'head')
The draws below stay inside these ranges and needn't reach their ends.
All inputs are finite; a program needn't handle non-finite values.
Results may differ from the reference program's by a relative error of at most 0.0057.
Values sent between devices are 32-bit elements; how exact they have to be, the bound alone decides.
A program may use at most 128 MiB of HBM per device.

```python
import math
import jax
import jax.numpy as jnp
from jax import lax

D = 6144
HEADS = 48
DH = 128
GROUP = 256
TOKENS = 4096


def draw_attn_out(key, part):
    first, second, third = jax.random.split(key, 3)
    head_of = jnp.arange(D) // DH
    rising = 0.6 * 3.0 ** (head_of.astype(jnp.float32) / max(HEADS - 1, 1))
    column = jnp.exp(jax.random.uniform(second, (D,), minval=math.log(0.3), maxval=math.log(3.0)))
    row_scale = jnp.exp(jax.random.uniform(third, (TOKENS, 1), minval=math.log(0.4), maxval=math.log(4.0)))
    base = jnp.clip(jax.random.normal(first, (TOKENS, D)), -5.0, 5.0)
    vals = base * rising * column * row_scale
    return vals.astype(jnp.float32).astype(jnp.bfloat16)


def block_levels(rng, shape, shards, low, top_value):
    def one(dim, shards_of):
        heights = jax.random.uniform(jax.random.fold_in(jax.random.fold_in(rng, 6), dim), (shards_of,), jnp.float32, low / len(shards), top_value / len(shards))
        return jnp.repeat(jnp.exp(heights), shape[dim] // shards_of).reshape((-1,) + (1,) * (len(shape) - dim - 1))

    factor_of = one(*shards[0])
    for cut in shards[1:]:
        factor_of = factor_of * one(*cut)
    return factor_of


def centred(own_key, dims, deviation, limit, pieces=(), dtype=jnp.bfloat16):
    values = jax.random.normal(own_key, dims, jnp.float32) * deviation
    if len(pieces) > 0:
        values = block_levels(own_key, dims, pieces, -0.22, 0.18) * values
    return jnp.clip(values, min=-limit, max=limit).astype(dtype)


def setup_inputs(seed: int = 0) -> dict:
    key_of = jax.random.split(jax.random.key(seed), 7)
    return {
        "queries": centred(key_of[0], (TOKENS, D), 1.0, 6.0, ((0, 8), (1, 4))),
        "keys": centred(key_of[1], (TOKENS, D), 1.0, 6.0, ((0, 8), (1, 4))),
        "values": centred(key_of[2], (TOKENS, D), 1.0, 6.0, ((0, 8), (1, 4))),
        "attn_out": draw_attn_out(jax.random.fold_in(key_of[6], 71), 0),
        "out_grad": centred(key_of[4], (TOKENS, D), 1.0, 6.0, ((0, 8), (1, 4))),
        "norm_gain": jnp.clip(jnp.exp(math.log(2.0) - 1.3862944 * jax.random.uniform(key_of[5], (D,), jnp.float32) ** block_levels(key_of[5], (D,), ((0, 4),), -0.2, 0.2)), 0.5, 2.0),
    }


EPS = 1e-06

def to_half(x):
    return lax.optimization_barrier(x.astype(jnp.bfloat16)).astype(jnp.float32)

def reference(queries, keys, values, attn_out, out_grad, norm_gain):
    outf = attn_out.astype(jnp.float32)
    scaled = norm_gain[None, :].astype(jnp.float32) * out_grad.astype(jnp.float32)
    square_sum = lax.optimization_barrier(jnp.sum(outf * outf, axis=-1))
    cross_sum = lax.optimization_barrier(jnp.sum(scaled * outf, axis=-1))
    rms = jnp.sqrt(square_sum / D + EPS)
    grad_out = (scaled / rms[:, None] - outf * (cross_sum / (D * rms ** 3))[:, None]).astype(jnp.bfloat16)
    blocks = TOKENS // GROUP
    shape = (blocks, GROUP, HEADS, DH)
    qs = queries.reshape(shape)
    ks = keys.reshape(shape)
    vs = values.reshape(shape)
    gs = grad_out.reshape(shape)
    causal = jnp.arange(GROUP)[:, None] >= jnp.arange(GROUP)[None, :]
    factor = 1.0 / math.sqrt(DH * TOKENS)

    def forward(state, items):
        qb, kb, vb, gb = [a.astype(jnp.float32) for a in items]
        prods = jnp.einsum('tnj,snj->nts', gb, vb)
        prods = to_half(jnp.where(causal[None], prods, 0.0))
        grad = jnp.einsum('nts,sni->tni', prods, kb) + jnp.einsum('tnj,nij->tni', gb, to_half(state))
        state = state + jnp.einsum('tni,tnj->nij', kb, vb)
        return (state, (grad * factor).astype(jnp.bfloat16))

    def backward(state, items):
        qb, kb, vb, gb = [a.astype(jnp.float32) for a in items]
        scores = to_half(jnp.where(causal[None], jnp.einsum('tni,sni->nts', qb, kb), 0.0))
        prods = to_half(jnp.where(causal[None], jnp.einsum('tnj,snj->nts', gb, vb), 0.0))
        half_state = to_half(state)
        kgrad = jnp.einsum('nts,tni->sni', prods, qb) + jnp.einsum('snj,nij->sni', vb, half_state)
        vgrad = jnp.einsum('nts,tnj->snj', scores, gb) + jnp.einsum('sni,nij->snj', kb, half_state)
        state = state + jnp.einsum('tni,tnj->nij', qb, gb)
        return (state, ((kgrad * factor).astype(jnp.bfloat16), (vgrad * factor).astype(jnp.bfloat16)))
    start = jnp.zeros((HEADS, DH, DH), jnp.float32)
    carry, qgrad = lax.scan(forward, start, (qs, ks, vs, gs))
    carry, pair = lax.scan(backward, start, (qs, ks, vs, gs), reverse=True)
    kgrad, vgrad = pair
    return (qgrad.reshape(TOKENS, D), kgrad.reshape(TOKENS, D), vgrad.reshape(TOKENS, D))
```

```python
import functools
import math

import jax
import jax.numpy as jnp
from jax import lax
from jax.experimental import pallas as pl
from jax.experimental.pallas import tpu as pltpu
from jax.sharding import PartitionSpec as P

DH = 128
GROUP = 256
EPS = 1e-06
MESH = pl.DeviceIdType.MESH
F32 = jnp.float32
BF16 = jnp.bfloat16
LAG = 2


def dot(a, b, ca, cb):
    return lax.dot_general(a, b, (((ca,), (cb,)), ((), ())), preferred_element_type=F32)


def split_seq(count):
    inner = 1
    while inner * inner * 4 <= count:
        inner *= 2
    while count % inner:
        inner //= 2
    return count // inner, inner


def kernel(
    cfg,
    q_hbm, k_hbm, v_hbm, o_hbm, d_hbm, gain_ref,
    qg_out, kg_out, vg_out,
    q_ref, k_ref, v_ref, o_ref, d_ref,
    acc_q, acc_k, acc_v, terms, slots, zin, inc, sums,
    load_sem, sum_send, sum_recv, y_send, y_recv, z_send, z_recv,
):
    zs, ys, hs, heads, ch, raw, rows, full_width, factor = cfg
    n = heads // ch
    blocks = rows // GROUP
    seq = lax.axis_index("seq")
    mine = lax.axis_index("head")
    z = seq // ys
    y = seq % ys
    hops = (z, zs - 1 - z)

    loads = [
        pltpu.make_async_copy(src, dst, load_sem.at[i])
        for i, (src, dst) in enumerate(
            ((k_hbm, k_ref), (v_hbm, v_ref), (o_hbm, o_ref), (d_hbm, d_ref), (q_hbm, q_ref))
        )
    ]
    for load in loads:
        load.start()

    barrier = pltpu.get_barrier_semaphore()

    def greet(s, h):
        pl.semaphore_signal(barrier, inc=1, device_id=(s, h), device_id_type=MESH)

    for d in range(1, hs):
        greet(seq, lax.rem(mine + d, hs))
    for d in range(1, ys):
        greet(z * ys + lax.rem(y + d, ys), mine)

    @pl.when(z > 0)
    def _():
        greet(seq - ys, mine)

    @pl.when(z < zs - 1)
    def _():
        greet(seq + ys, mine)

    for kind in range(2):

        @pl.when(hops[kind] == 0)
        def _():
            zin[kind] = jnp.zeros_like(zin[kind])

    def chunk(c):
        return pl.ds(c * ch, ch)

    def lanes(h):
        return pl.ds(pl.multiple_of(h * DH, DH), DH)

    def toks(b):
        return slice(b * GROUP, (b + 1) * GROUP)

    def y_copy(kind, src, c, d):
        other = lax.rem(y + d, ys)
        return pltpu.make_async_remote_copy(
            src_ref=src.at[chunk(c)],
            dst_ref=slots.at[kind, y, chunk(c)],
            send_sem=y_send.at[kind, d - 1, c],
            recv_sem=y_recv.at[kind, y, c],
            device_id=(z * ys + other, mine),
            device_id_type=MESH,
        )

    def y_arrive(kind, c, d):
        other = lax.rem(y + d, ys)
        pltpu.make_async_remote_copy(
            src_ref=slots.at[kind, other, chunk(c)],
            dst_ref=slots.at[kind, other, chunk(c)],
            send_sem=y_send.at[kind, d - 1, c],
            recv_sem=y_recv.at[kind, other, c],
            device_id=(z * ys + other, mine),
            device_id_type=MESH,
        ).wait_recv()

    def z_copy(kind, c):
        return pltpu.make_async_remote_copy(
            src_ref=inc.at[kind, chunk(c)],
            dst_ref=zin.at[kind, chunk(c)],
            send_sem=z_send.at[kind, c],
            recv_sem=z_recv.at[kind, c],
            device_id=(seq + (ys if kind == 0 else -ys), mine),
            device_id_type=MESH,
        )

    def later(kind, other):
        return other > y if kind == 0 else other < y

    def own_terms(kind, a_ref, b_ref):
        def one(c, carry):
            for i in range(ch):
                h = c * ch + i
                total = None
                for b in range(blocks):
                    part = dot(a_ref[toks(b), lanes(h)], b_ref[toks(b), lanes(h)], 0, 0)
                    terms[kind, b, h] = part
                    total = part if total is None else total + part
                slots[kind, y, h] = total

            @pl.when(c < raw)
            def _():
                for d in range(1, ys):
                    y_copy(kind, slots.at[kind, y], c, d).start()

            return carry

        lax.fori_loop(0, n, one, 0)

    def step(kind, t):
        place = t - hops[kind]

        @pl.when((place >= 0) & (place < n))
        def _():
            c = lax.rem(place + raw, n)

            @pl.when(hops[kind] > 0)
            def _():
                z_copy(kind, c).wait_recv()

            @pl.when(place >= n - raw)
            def _():
                for d in range(1, ys):
                    y_arrive(kind, c, d)
                total = zin[kind, chunk(c)]
                for s in range(ys):
                    total = total + slots[kind, s, chunk(c)]
                inc[kind, chunk(c)] = total

            @pl.when(place < n - raw)
            def _():
                inc[kind, chunk(c)] = zin[kind, chunk(c)] + slots[kind, y, chunk(c)]
                for d in range(1, ys):
                    other = lax.rem(y + d, ys)

                    @pl.when(later(kind, other))
                    def _():
                        y_copy(kind, inc.at[kind], c, d).start()

                    @pl.when(jnp.logical_not(later(kind, other)))
                    def _():
                        y_copy(kind, zin.at[kind], c, d).start()

            @pl.when(hops[kind] < zs - 1)
            def _():
                z_copy(kind, c).start()

    loads[0].wait()
    loads[1].wait()
    peers = hs - 1 + ys - 1 + jnp.where(z > 0, 1, 0) + jnp.where(z < zs - 1, 1, 0)
    pl.semaphore_wait(barrier, peers)
    own_terms(0, k_ref, v_ref)
    step(0, 0)

    loads[2].wait()
    loads[3].wait()
    tile = 128
    for r in range(rows // tile):
        rs = slice(r * tile, (r + 1) * tile)

        def partial(h, carry):
            sq, cr = carry
            of = o_ref[rs, lanes(h)].astype(F32)
            sc = gain_ref[0:1, lanes(h)] * d_ref[rs, lanes(h)].astype(F32)
            return sq + of * of, cr + sc * of

        zero = jnp.zeros((tile, DH), F32)
        sq, cr = lax.fori_loop(0, heads, partial, (zero, zero))
        sq = jnp.sum(sq.T, axis=0, keepdims=True)
        cr = jnp.sum(cr.T, axis=0, keepdims=True)
        sums[mine, 0:4, rs] = jnp.broadcast_to(sq, (4, tile))
        sums[mine, 4:8, rs] = jnp.broadcast_to(cr, (4, tile))

    def sum_copy(slot, d):
        return pltpu.make_async_remote_copy(
            src_ref=sums.at[slot],
            dst_ref=sums.at[slot],
            send_sem=sum_send.at[d - 1],
            recv_sem=sum_recv.at[slot],
            device_id=(seq, lax.rem(mine + d, hs)),
            device_id_type=MESH,
        )

    for d in range(1, hs):
        sum_copy(mine, d).start()
    for t in range(1, LAG):
        step(0, t)
    for d in range(1, hs):
        sum_copy(lax.rem(mine + d, hs), d).wait_recv()
    total = sums[0]
    for s in range(1, hs):
        total = total + sums[s]
    rms = jnp.sqrt(total[0:1] / full_width + EPS)
    inv_row = 1.0 / rms
    coef_row = total[4:5] / (full_width * (rms * rms * rms))
    for r in range(rows // tile):
        rs = slice(r * tile, (r + 1) * tile)
        inv = jnp.broadcast_to(inv_row[:, rs], (tile, tile)).T
        coef = jnp.broadcast_to(coef_row[:, rs], (tile, tile)).T

        def normed(h, carry):
            of = o_ref[rs, lanes(h)].astype(F32)
            sc = gain_ref[0:1, lanes(h)] * d_ref[rs, lanes(h)].astype(F32)
            d_ref[rs, lanes(h)] = (sc * inv - of * coef).astype(BF16)
            return carry

        lax.fori_loop(0, heads, normed, 0)

    loads[4].wait()
    own_terms(1, q_ref, d_ref)

    def local(c):
        row = lax.broadcasted_iota(jnp.int32, (GROUP, GROUP), 0)
        col = lax.broadcasted_iota(jnp.int32, (GROUP, GROUP), 1)
        for i in range(ch):
            h = c * ch + i
            for b in range(blocks):
                qb = q_ref[toks(b), lanes(h)]
                kb = k_ref[toks(b), lanes(h)]
                vb = v_ref[toks(b), lanes(h)]
                gb = d_ref[toks(b), lanes(h)]
                prods = jnp.where(row >= col, dot(gb, vb, 1, 1), 0.0).astype(BF16)
                acc_q[toks(b), lanes(h)] = dot(prods, kb, 1, 0)
                prods_t = jnp.where(col >= row, dot(vb, gb, 1, 1), 0.0).astype(BF16)
                acc_k[toks(b), lanes(h)] = dot(prods_t, qb, 1, 0)
                scores_t = jnp.where(col >= row, dot(kb, qb, 1, 1), 0.0).astype(BF16)
                acc_v[toks(b), lanes(h)] = dot(scores_t, gb, 1, 0)

    def turn(t, carry):
        step(0, t)
        step(1, t - LAG)

        @pl.when(t - LAG < n)
        def _():
            local(t - LAG)

        return carry

    lax.fori_loop(LAG, n + zs - 1 + LAG, turn, 0)

    def finish(c, carry):
        @pl.when(c >= raw)
        def _():
            for kind in range(2):
                for d in range(1, ys):
                    y_arrive(kind, c, d)

        for i in range(ch):
            h = c * ch + i
            ends = []
            for kind in range(2):
                total = zin[kind, h]
                for d in range(1, ys):
                    other = lax.rem(y + d, ys)
                    used = jnp.logical_or(c >= raw, jnp.logical_not(later(kind, other)))
                    total = total + jnp.where(used, slots[kind, other, h], 0.0)
                ends.append(total)
            fwd, bwd = [ends[0]], [ends[1]]
            for b in range(blocks - 1):
                fwd.append(fwd[-1] + terms[0, b, h])
                bwd.insert(0, bwd[0] + terms[1, blocks - 1 - b, h])
            for b in range(blocks):
                at = (toks(b), lanes(h))
                kb, vb, gb = k_ref[at], v_ref[at], d_ref[at]
                fs, bs = fwd[b].astype(BF16), bwd[b].astype(BF16)
                qg_out[at] = ((acc_q[at] + dot(gb, fs, 1, 1)) * factor).astype(BF16)
                kg_out[at] = ((acc_k[at] + dot(vb, bs, 1, 1)) * factor).astype(BF16)
                vg_out[at] = ((acc_v[at] + dot(kb, bs, 1, 0)) * factor).astype(BF16)
        return carry

    lax.fori_loop(0, n, finish, 0)

    for d in range(1, hs):
        sum_copy(mine, d).wait_send()

    def sent(c, carry):
        for kind in range(2):
            for d in range(1, ys):
                y_copy(kind, inc.at[kind], c, d).wait_send()

            @pl.when(hops[kind] < zs - 1)
            def _():
                z_copy(kind, c).wait_send()

        return carry

    lax.fori_loop(0, n, sent, 0)


def shards(sizes, queries, keys, values, attn_out, out_grad, norm_gain):
    seqs, hs = sizes
    zs, ys = split_seq(seqs)
    rows, width = queries.shape
    heads = width // DH
    blocks = rows // GROUP
    ch = 2 if heads % 2 == 0 else 1
    n = heads // ch
    raw = n // 3
    factor = 1.0 / math.sqrt(DH * rows * seqs)
    cfg = (zs, ys, hs, heads, ch, raw, rows, width * hs, factor)
    big = pltpu.VMEM((rows, width), BF16)
    acc = pltpu.VMEM((rows, width), F32)
    state = (heads, DH, DH)
    out = jax.ShapeDtypeStruct((rows, width), BF16)
    dma = pltpu.SemaphoreType.DMA
    flops = 2 * heads * blocks * (6 * GROUP * GROUP * DH + 5 * GROUP * DH * DH)
    return pl.pallas_call(
        functools.partial(kernel, cfg),
        out_shape=(out, out, out),
        in_specs=[pl.BlockSpec(memory_space=pl.ANY)] * 5 + [pl.BlockSpec(memory_space=pltpu.VMEM)],
        out_specs=[pl.BlockSpec(memory_space=pltpu.VMEM)] * 3,
        scratch_shapes=[
            big, big, big, big, big,
            acc, acc, acc,
            pltpu.VMEM((2, blocks) + state, F32),
            pltpu.VMEM((2, ys) + state, F32),
            pltpu.VMEM((2,) + state, F32),
            pltpu.VMEM((2,) + state, F32),
            pltpu.VMEM((hs, 8, rows), F32),
            dma((5,)),
            dma((hs - 1,)),
            dma((hs,)),
            dma((2, ys - 1, n)),
            dma((2, ys, n)),
            dma((2, n)),
            dma((2, n)),
        ],
        cost_estimate=pl.CostEstimate(
            flops=flops, bytes_accessed=8 * rows * width * 2, transcendentals=0
        ),
        compiler_params=pltpu.CompilerParams(
            collective_id=0, has_side_effects=True, vmem_limit_bytes=42 * 1024 * 1024
        ),
    )(queries, keys, values, attn_out, out_grad, norm_gain[None, :])


def solution(mesh):
    sizes = (mesh.shape["seq"], mesh.shape["head"])
    spec = P("seq", "head")
    return jax.shard_map(
        functools.partial(shards, sizes),
        mesh=mesh,
        in_specs=(spec,) * 5 + (P("head"),),
        out_specs=(spec,) * 3,
        check_vma=False,
    )
```

```python
import functools
import math

import jax
import jax.numpy as jnp
from jax import lax
from jax.experimental import pallas as pl
from jax.experimental.pallas import tpu as pltpu
from jax.sharding import PartitionSpec as P

DH = 128
GROUP = 256
EPS = 1e-06
MESH = pl.DeviceIdType.MESH
F32 = jnp.float32
BF16 = jnp.bfloat16
LAG = 2
STORES = 4


def dot(a, b, ca, cb):
    return lax.dot_general(a, b, (((ca,), (cb,)), ((), ())), preferred_element_type=F32)


def split_seq(count):
    inner = 1
    while inner * inner * 4 <= count:
        inner *= 2
    while count % inner:
        inner //= 2
    return count // inner, inner


def kernel(
    cfg,
    q_hbm, k_hbm, v_hbm, o_hbm, d_hbm, gain_hbm,
    qg_out, kg_out, vg_out,
    q_ref, k_ref, v_ref, o_ref, d_ref, gain_ref,
    acc_q, acc_k, acc_v, terms, slots, zin, inc, sums,
    load_sem, sum_send, sum_recv, y_send, y_recv, z_send, z_recv,
):
    zs, ys, hs, heads, ch, raw, rows, full_width, factor = cfg
    n = heads // ch
    blocks = rows // GROUP
    seq = lax.axis_index("seq")
    mine = lax.axis_index("head")
    z = seq // ys
    y = seq % ys
    hops = (z, zs - 1 - z)
    steps = (zs - 1) * 3 // 2 + LAG + n

    loads = [
        pltpu.make_async_copy(src, dst, load_sem.at[i])
        for i, (src, dst) in enumerate(
            ((k_hbm, k_ref), (v_hbm, v_ref), (o_hbm, o_ref), (d_hbm, d_ref), (q_hbm, q_ref))
        )
    ]
    for load in loads:
        load.start()
    gain_load = pltpu.make_async_copy(gain_hbm, gain_ref, load_sem.at[5])
    gain_load.start()

    barrier = pltpu.get_barrier_semaphore()

    def greet(s, h):
        pl.semaphore_signal(barrier, inc=1, device_id=(s, h), device_id_type=MESH)

    for d in range(1, hs):
        greet(seq, lax.rem(mine + d, hs))
    for d in range(1, ys):
        greet(z * ys + lax.rem(y + d, ys), mine)

    @pl.when(z > 0)
    def _():
        greet(seq - ys, mine)

    @pl.when(z < zs - 1)
    def _():
        greet(seq + ys, mine)

    for kind in range(2):

        @pl.when(hops[kind] == 0)
        def _():
            zin[kind] = jnp.zeros_like(zin[kind])

    def chunk(c):
        return pl.ds(c * ch, ch)

    def lanes(h):
        return pl.ds(pl.multiple_of(h * DH, DH), DH)

    def toks(b):
        return slice(b * GROUP, (b + 1) * GROUP)

    def y_copy(kind, src, c, d):
        other = lax.rem(y + d, ys)
        return pltpu.make_async_remote_copy(
            src_ref=src.at[chunk(c)],
            dst_ref=slots.at[kind, y, chunk(c)],
            send_sem=y_send.at[kind, d - 1, c],
            recv_sem=y_recv.at[kind, y, c],
            device_id=(z * ys + other, mine),
            device_id_type=MESH,
        )

    def y_arrive(kind, c, d):
        other = lax.rem(y + d, ys)
        pltpu.make_async_remote_copy(
            src_ref=slots.at[kind, other, chunk(c)],
            dst_ref=slots.at[kind, other, chunk(c)],
            send_sem=y_send.at[kind, d - 1, c],
            recv_sem=y_recv.at[kind, other, c],
            device_id=(z * ys + other, mine),
            device_id_type=MESH,
        ).wait_recv()

    def z_copy(kind, c):
        return pltpu.make_async_remote_copy(
            src_ref=inc.at[kind, chunk(c)],
            dst_ref=zin.at[kind, chunk(c)],
            send_sem=z_send.at[kind, c],
            recv_sem=z_recv.at[kind, c],
            device_id=(seq + (ys if kind == 0 else -ys), mine),
            device_id_type=MESH,
        )

    def later(kind, other):
        return other > y if kind == 0 else other < y

    def own_terms(kind, a_ref, b_ref):
        def one(c, carry):
            for i in range(ch):
                h = c * ch + i
                total = None
                for b in range(blocks):
                    part = dot(a_ref[toks(b), lanes(h)], b_ref[toks(b), lanes(h)], 0, 0)
                    terms[kind, b, h] = part
                    total = part if total is None else total + part
                slots[kind, y, h] = total

            @pl.when(c < raw)
            def _():
                for d in range(1, ys):
                    y_copy(kind, slots.at[kind, y], c, d).start()

            return carry

        lax.fori_loop(0, n, one, 0)

    def step(kind, place):
        @pl.when((place >= 0) & (place < n))
        def _():
            c = lax.rem(place + raw, n)

            @pl.when(hops[kind] > 0)
            def _():
                z_copy(kind, c).wait_recv()

            @pl.when(place >= n - raw)
            def _():
                for d in range(1, ys):
                    y_arrive(kind, c, d)
                total = zin[kind, chunk(c)]
                for s in range(ys):
                    total = total + slots[kind, s, chunk(c)]
                inc[kind, chunk(c)] = total

            @pl.when(place < n - raw)
            def _():
                inc[kind, chunk(c)] = zin[kind, chunk(c)] + slots[kind, y, chunk(c)]
                for d in range(1, ys):
                    other = lax.rem(y + d, ys)

                    @pl.when(later(kind, other))
                    def _():
                        y_copy(kind, inc.at[kind], c, d).start()

                    @pl.when(jnp.logical_not(later(kind, other)) & (hops[kind] > 0))
                    def _():
                        y_copy(kind, zin.at[kind], c, d).start()

            @pl.when(hops[kind] < zs - 1)
            def _():
                z_copy(kind, c).start()

    def start(kind):
        first = hops[kind] * 3 // 2 + kind * LAG
        return jnp.where(hops[kind] == 0, steps, first)

    loads[0].wait()
    loads[1].wait()
    peers = hs - 1 + ys - 1 + jnp.where(z > 0, 1, 0) + jnp.where(z < zs - 1, 1, 0)
    pl.semaphore_wait(barrier, peers)
    own_terms(0, k_ref, v_ref)
    def ends(kind):
        @pl.when(hops[kind] == 0)
        def _():
            lax.fori_loop(0, n, lambda p, carry: (step(kind, p), carry)[1], 0)

    ends(0)
    step(0, 0 - start(0))

    loads[2].wait()
    loads[3].wait()
    gain_load.wait()
    tile = 128
    for r in range(rows // tile):
        rs = slice(r * tile, (r + 1) * tile)

        def partial(h, carry):
            sq, cr = carry
            of = o_ref[rs, lanes(h)].astype(F32)
            sc = gain_ref[lanes(h)][None, :] * d_ref[rs, lanes(h)].astype(F32)
            return sq + of * of, cr + sc * of

        zero = jnp.zeros((tile, DH), F32)
        sq, cr = lax.fori_loop(0, heads, partial, (zero, zero))
        sq = jnp.sum(sq.T, axis=0, keepdims=True)
        cr = jnp.sum(cr.T, axis=0, keepdims=True)
        sums[mine, 0:4, rs] = jnp.broadcast_to(sq, (4, tile))
        sums[mine, 4:8, rs] = jnp.broadcast_to(cr, (4, tile))

    def sum_copy(slot, d):
        return pltpu.make_async_remote_copy(
            src_ref=sums.at[slot],
            dst_ref=sums.at[slot],
            send_sem=sum_send.at[d - 1],
            recv_sem=sum_recv.at[slot],
            device_id=(seq, lax.rem(mine + d, hs)),
            device_id_type=MESH,
        )

    for d in range(1, hs):
        sum_copy(mine, d).start()
    for t in range(1, LAG):
        step(0, t - start(0))
    for d in range(1, hs):
        sum_copy(lax.rem(mine + d, hs), d).wait_recv()
    total = sums[0]
    for s in range(1, hs):
        total = total + sums[s]
    rms = jnp.sqrt(total[0:1] / full_width + EPS)
    inv_row = 1.0 / rms
    coef_row = total[4:5] / (full_width * (rms * rms * rms))
    for r in range(rows // tile):
        rs = slice(r * tile, (r + 1) * tile)
        inv = jnp.broadcast_to(inv_row[:, rs], (tile, tile)).T
        coef = jnp.broadcast_to(coef_row[:, rs], (tile, tile)).T

        def normed(h, carry):
            of = o_ref[rs, lanes(h)].astype(F32)
            sc = gain_ref[lanes(h)][None, :] * d_ref[rs, lanes(h)].astype(F32)
            d_ref[rs, lanes(h)] = (sc * inv - of * coef).astype(BF16)
            return carry

        lax.fori_loop(0, heads, normed, 0)

    loads[4].wait()
    own_terms(1, q_ref, d_ref)
    ends(1)

    def local(c):
        row = lax.broadcasted_iota(jnp.int32, (GROUP, GROUP), 0)
        col = lax.broadcasted_iota(jnp.int32, (GROUP, GROUP), 1)
        for i in range(ch):
            h = c * ch + i
            for b in range(blocks):
                qb = q_ref[toks(b), lanes(h)]
                kb = k_ref[toks(b), lanes(h)]
                vb = v_ref[toks(b), lanes(h)]
                gb = d_ref[toks(b), lanes(h)]
                prods = jnp.where(row >= col, dot(gb, vb, 1, 1), 0.0).astype(BF16)
                acc_q[toks(b), lanes(h)] = dot(prods, kb, 1, 0)
                prods_t = jnp.where(col >= row, dot(vb, gb, 1, 1), 0.0).astype(BF16)
                acc_k[toks(b), lanes(h)] = dot(prods_t, qb, 1, 0)
                scores_t = jnp.where(col >= row, dot(kb, qb, 1, 1), 0.0).astype(BF16)
                acc_v[toks(b), lanes(h)] = dot(scores_t, gb, 1, 0)

    def turn(t, carry):
        step(0, t - start(0))
        step(1, t - start(1))

        @pl.when(t - LAG < n)
        def _():
            local(t - LAG)

        return carry

    lax.fori_loop(LAG, steps, turn, 0)

    def finish(c, carry):
        @pl.when(c >= raw)
        def _():
            for kind in range(2):
                for d in range(1, ys):
                    other = lax.rem(y + d, ys)

                    @pl.when(jnp.logical_not(later(kind, other)) | (hops[kind] > 0))
                    def _():
                        y_arrive(kind, c, d)

        for i in range(ch):
            h = c * ch + i
            ends = []
            for kind in range(2):
                total = zin[kind, h]
                for d in range(1, ys):
                    other = lax.rem(y + d, ys)
                    used = jnp.logical_not(later(kind, other)) | ((c >= raw) & (hops[kind] > 0))
                    total = total + jnp.where(used, slots[kind, other, h], 0.0)
                ends.append(total)
            fwd, bwd = [ends[0]], [ends[1]]
            for b in range(blocks - 1):
                fwd.append(fwd[-1] + terms[0, b, h])
                bwd.insert(0, bwd[0] + terms[1, blocks - 1 - b, h])
            for b in range(blocks):
                at = (toks(b), lanes(h))
                kb, vb, gb = k_ref[at], v_ref[at], d_ref[at]
                fs, bs = fwd[b].astype(BF16), bwd[b].astype(BF16)
                qg_out[at] = ((acc_q[at] + dot(gb, fs, 1, 1)) * factor).astype(BF16)
                kg_out[at] = ((acc_k[at] + dot(vb, bs, 1, 1)) * factor).astype(BF16)
                vg_out[at] = ((acc_v[at] + dot(kb, bs, 1, 0)) * factor).astype(BF16)
        return carry

    lax.fori_loop(0, n, finish, 0)

    for d in range(1, hs):
        sum_copy(mine, d).wait_send()

    def sent(c, carry):
        for kind in range(2):
            for d in range(1, ys):
                other = lax.rem(y + d, ys)

                @pl.when(later(kind, other) | (c < raw) | (hops[kind] > 0))
                def _():
                    y_copy(kind, inc.at[kind], c, d).wait_send()

            @pl.when(hops[kind] < zs - 1)
            def _():
                z_copy(kind, c).wait_send()

        return carry

    lax.fori_loop(0, n, sent, 0)


def store_kernel(a, b, c, a_out, b_out, c_out, sem):
    part = a.shape[0] // STORES
    copies = []
    for i in range(STORES):
        at = slice(i * part, (i + 1) * part)
        for j, (src, dst) in enumerate(((a, a_out), (b, b_out), (c, c_out))):
            copies.append(pltpu.make_async_copy(src.at[at], dst.at[at], sem.at[j, i]))
    for copy in copies:
        copy.start()
    for copy in copies:
        copy.wait()


def shards(sizes, queries, keys, values, attn_out, out_grad, norm_gain):
    seqs, hs = sizes
    zs, ys = split_seq(seqs)
    rows, width = queries.shape
    heads = width // DH
    blocks = rows // GROUP
    ch = 2 if heads % 2 == 0 else 1
    n = heads // ch
    raw = n // 3
    factor = 1.0 / math.sqrt(DH * rows * seqs)
    cfg = (zs, ys, hs, heads, ch, raw, rows, width * hs, factor)
    big = pltpu.VMEM((rows, width), BF16)
    acc = pltpu.VMEM((rows, width), F32)
    state = (heads, DH, DH)
    out = jax.ShapeDtypeStruct((rows, width), BF16)
    dma = pltpu.SemaphoreType.DMA
    flops = 2 * heads * blocks * (6 * GROUP * GROUP * DH + 5 * GROUP * DH * DH)
    held = pl.pallas_call(
        functools.partial(kernel, cfg),
        out_shape=(out, out, out),
        in_specs=[pl.BlockSpec(memory_space=pltpu.HBM)] * 6,
        out_specs=[pl.BlockSpec(memory_space=pltpu.VMEM)] * 3,
        scratch_shapes=[
            big, big, big, big, big,
            pltpu.VMEM((width,), F32),
            acc, acc, acc,
            pltpu.VMEM((2, blocks) + state, F32),
            pltpu.VMEM((2, ys) + state, F32),
            pltpu.VMEM((2,) + state, F32),
            pltpu.VMEM((2,) + state, F32),
            pltpu.VMEM((hs, 8, rows), F32),
            dma((6,)),
            dma((hs - 1,)),
            dma((hs,)),
            dma((2, ys - 1, n)),
            dma((2, ys, n)),
            dma((2, n)),
            dma((2, n)),
        ],
        cost_estimate=pl.CostEstimate(
            flops=flops, bytes_accessed=8 * rows * width * 2, transcendentals=0
        ),
        compiler_params=pltpu.CompilerParams(
            collective_id=0, has_side_effects=True, vmem_limit_bytes=42 * 1024 * 1024
        ),
    )(*[
        pltpu.with_memory_space_constraint(x, pltpu.HBM)
        for x in (queries, keys, values, attn_out, out_grad, norm_gain)
    ])
    return pl.pallas_call(
        store_kernel,
        out_shape=(out, out, out),
        in_specs=[pl.BlockSpec(memory_space=pltpu.VMEM)] * 3,
        out_specs=[pl.BlockSpec(memory_space=pltpu.HBM)] * 3,
        scratch_shapes=[dma((3, STORES))],
        cost_estimate=pl.CostEstimate(
            flops=0, bytes_accessed=3 * rows * width * 2, transcendentals=0
        ),
    )(*held)


def solution(mesh):
    sizes = (mesh.shape["seq"], mesh.shape["head"])
    spec = P("seq", "head")
    return jax.shard_map(
        functools.partial(shards, sizes),
        mesh=mesh,
        in_specs=(spec,) * 5 + (P("head"),),
        out_specs=(spec,) * 3,
        check_vma=False,
    )
```

```python
import functools
import math

import jax
import jax.numpy as jnp
from jax import lax
from jax.experimental import pallas as pl
from jax.experimental.pallas import tpu as pltpu
from jax.sharding import PartitionSpec as P

DH = 128
GROUP = 256
EPS = 1e-06
MESH = pl.DeviceIdType.MESH
F32 = jnp.float32
BF16 = jnp.bfloat16
LAG = 4
EARLY = 3
HOP = 2
SETTLE = 3
STORES = 4


def dot(a, b, ca, cb):
    return lax.dot_general(a, b, (((ca,), (cb,)), ((), ())), preferred_element_type=F32)


def split_seq(count):
    inner = 1
    while inner * inner * 4 <= count:
        inner *= 2
    while count % inner:
        inner //= 2
    return count // inner, inner


def kernel(
    cfg,
    q_hbm, k_hbm, v_hbm, o_hbm, d_hbm, gain_hbm,
    qg_out, kg_out, vg_out,
    q_ref, k_ref, v_ref, o_ref, d_ref, gain_ref,
    acc_q, acc_k, acc_v, terms, slots, zin, inc, sums,
    load_sem, sum_send, sum_recv, y_send, y_recv, z_send, z_recv,
):
    zs, ys, hs, heads, ch, raw, rows, full_width, factor = cfg
    n = heads // ch
    blocks = rows // GROUP
    seq = lax.axis_index("seq")
    mine = lax.axis_index("head")
    z = seq // ys
    y = seq % ys
    hops = (z, zs - 1 - z)
    steps = (zs - 1) * HOP + LAG + n

    loads = [
        pltpu.make_async_copy(src, dst, load_sem.at[i])
        for i, (src, dst) in enumerate(
            ((k_hbm, k_ref), (v_hbm, v_ref), (o_hbm, o_ref), (d_hbm, d_ref), (q_hbm, q_ref))
        )
    ]
    for load in loads:
        load.start()
    gain_load = pltpu.make_async_copy(gain_hbm, gain_ref, load_sem.at[5])
    gain_load.start()

    barrier = pltpu.get_barrier_semaphore()

    def greet(s, h):
        pl.semaphore_signal(barrier, inc=1, device_id=(s, h), device_id_type=MESH)

    for d in range(1, hs):
        greet(seq, lax.rem(mine + d, hs))
    for d in range(1, ys):
        greet(z * ys + lax.rem(y + d, ys), mine)

    @pl.when(z > 0)
    def _():
        greet(seq - ys, mine)

    @pl.when(z < zs - 1)
    def _():
        greet(seq + ys, mine)

    for kind in range(2):

        @pl.when(hops[kind] == 0)
        def _():
            zin[kind] = jnp.zeros_like(zin[kind])

    def chunk(c):
        return pl.ds(c * ch, ch)

    def lanes(h):
        return pl.ds(pl.multiple_of(h * DH, DH), DH)

    def toks(b):
        return slice(b * GROUP, (b + 1) * GROUP)

    def y_copy(kind, src, c, d):
        other = lax.rem(y + d, ys)
        return pltpu.make_async_remote_copy(
            src_ref=src.at[chunk(c)],
            dst_ref=slots.at[kind, y, chunk(c)],
            send_sem=y_send.at[kind, d - 1, c],
            recv_sem=y_recv.at[kind, y, c],
            device_id=(z * ys + other, mine),
            device_id_type=MESH,
        )

    def y_arrive(kind, c, d):
        other = lax.rem(y + d, ys)
        pltpu.make_async_remote_copy(
            src_ref=slots.at[kind, other, chunk(c)],
            dst_ref=slots.at[kind, other, chunk(c)],
            send_sem=y_send.at[kind, d - 1, c],
            recv_sem=y_recv.at[kind, other, c],
            device_id=(z * ys + other, mine),
            device_id_type=MESH,
        ).wait_recv()

    def z_copy(kind, c):
        return pltpu.make_async_remote_copy(
            src_ref=inc.at[kind, chunk(c)],
            dst_ref=zin.at[kind, chunk(c)],
            send_sem=z_send.at[kind, c],
            recv_sem=z_recv.at[kind, c],
            device_id=(seq + (ys if kind == 0 else -ys), mine),
            device_id_type=MESH,
        )

    def later(kind, other):
        return other > y if kind == 0 else other < y

    def own_terms(kind, a_ref, b_ref):
        def one(c, carry):
            for i in range(ch):
                h = c * ch + i
                total = None
                for b in range(blocks):
                    part = dot(a_ref[toks(b), lanes(h)], b_ref[toks(b), lanes(h)], 0, 0)
                    terms[kind, b, h] = part
                    total = part if total is None else total + part
                slots[kind, y, h] = total

            @pl.when(c < raw)
            def _():
                for d in range(1, ys):
                    y_copy(kind, slots.at[kind, y], c, d).start()

            return carry

        lax.fori_loop(0, n, one, 0)

    def step(kind, place):
        @pl.when((place >= 0) & (place < n))
        def _():
            c = lax.rem(place + raw, n)

            @pl.when(hops[kind] > 0)
            def _():
                z_copy(kind, c).wait_recv()

            @pl.when(place >= n - raw)
            def _():
                for d in range(1, ys):
                    y_arrive(kind, c, d)
                total = zin[kind, chunk(c)]
                for s in range(ys):
                    total = total + slots[kind, s, chunk(c)]
                inc[kind, chunk(c)] = total

            @pl.when(place < n - raw)
            def _():
                inc[kind, chunk(c)] = zin[kind, chunk(c)] + slots[kind, y, chunk(c)]
                for d in range(1, ys):
                    other = lax.rem(y + d, ys)

                    @pl.when(later(kind, other))
                    def _():
                        y_copy(kind, inc.at[kind], c, d).start()

                    @pl.when(jnp.logical_not(later(kind, other)) & (hops[kind] > 0))
                    def _():
                        y_copy(kind, zin.at[kind], c, d).start()

            @pl.when(hops[kind] < zs - 1)
            def _():
                z_copy(kind, c).start()

    def start(kind):
        first = hops[kind] * HOP + kind * LAG
        return jnp.where(hops[kind] == 0, steps + SETTLE, first)

    loads[0].wait()
    loads[1].wait()
    peers = hs - 1 + ys - 1 + jnp.where(z > 0, 1, 0) + jnp.where(z < zs - 1, 1, 0)
    pl.semaphore_wait(barrier, peers)
    own_terms(0, k_ref, v_ref)
    def ends(kind):
        @pl.when(hops[kind] == 0)
        def _():
            lax.fori_loop(0, n, lambda p, carry: (step(kind, p), carry)[1], 0)

    ends(0)
    step(0, 0 - start(0))

    loads[2].wait()
    loads[3].wait()
    gain_load.wait()
    tile = 128
    for r in range(rows // tile):
        rs = slice(r * tile, (r + 1) * tile)

        def partial(h, carry):
            sq, cr = carry
            of = o_ref[rs, lanes(h)].astype(F32)
            sc = gain_ref[lanes(h)][None, :] * d_ref[rs, lanes(h)].astype(F32)
            return sq + of * of, cr + sc * of

        zero = jnp.zeros((tile, DH), F32)
        sq, cr = lax.fori_loop(0, heads, partial, (zero, zero))
        sq = jnp.sum(sq.T, axis=0, keepdims=True)
        cr = jnp.sum(cr.T, axis=0, keepdims=True)
        sums[mine, 0:4, rs] = jnp.broadcast_to(sq, (4, tile))
        sums[mine, 4:8, rs] = jnp.broadcast_to(cr, (4, tile))

    def sum_copy(slot, d):
        return pltpu.make_async_remote_copy(
            src_ref=sums.at[slot],
            dst_ref=sums.at[slot],
            send_sem=sum_send.at[d - 1],
            recv_sem=sum_recv.at[slot],
            device_id=(seq, lax.rem(mine + d, hs)),
            device_id_type=MESH,
        )

    for d in range(1, hs):
        sum_copy(mine, d).start()
    for t in range(1, EARLY):
        step(0, t - start(0))
    for d in range(1, hs):
        sum_copy(lax.rem(mine + d, hs), d).wait_recv()
    total = sums[0]
    for s in range(1, hs):
        total = total + sums[s]
    rms = jnp.sqrt(total[0:1] / full_width + EPS)
    inv_row = 1.0 / rms
    coef_row = total[4:5] / (full_width * (rms * rms * rms))
    for r in range(rows // tile):
        rs = slice(r * tile, (r + 1) * tile)
        inv = jnp.broadcast_to(inv_row[:, rs], (tile, tile)).T
        coef = jnp.broadcast_to(coef_row[:, rs], (tile, tile)).T

        def normed(h, carry):
            of = o_ref[rs, lanes(h)].astype(F32)
            sc = gain_ref[lanes(h)][None, :] * d_ref[rs, lanes(h)].astype(F32)
            d_ref[rs, lanes(h)] = (sc * inv - of * coef).astype(BF16)
            return carry

        lax.fori_loop(0, heads, normed, 0)

    loads[4].wait()
    own_terms(1, q_ref, d_ref)
    ends(1)

    def local(c):
        row = lax.broadcasted_iota(jnp.int32, (GROUP, GROUP), 0)
        col = lax.broadcasted_iota(jnp.int32, (GROUP, GROUP), 1)
        for i in range(ch):
            h = c * ch + i
            for b in range(blocks):
                qb = q_ref[toks(b), lanes(h)]
                kb = k_ref[toks(b), lanes(h)]
                vb = v_ref[toks(b), lanes(h)]
                gb = d_ref[toks(b), lanes(h)]
                prods = jnp.where(row >= col, dot(gb, vb, 1, 1), 0.0).astype(BF16)
                acc_q[toks(b), lanes(h)] = dot(prods, kb, 1, 0)
                prods_t = jnp.where(col >= row, dot(vb, gb, 1, 1), 0.0).astype(BF16)
                acc_k[toks(b), lanes(h)] = dot(prods_t, qb, 1, 0)
                scores_t = jnp.where(col >= row, dot(kb, qb, 1, 1), 0.0).astype(BF16)
                acc_v[toks(b), lanes(h)] = dot(scores_t, gb, 1, 0)

    def finish(c):
        @pl.when(c >= raw)
        def _():
            for kind in range(2):
                for d in range(1, ys):
                    other = lax.rem(y + d, ys)

                    @pl.when(jnp.logical_not(later(kind, other)) | (hops[kind] > 0))
                    def _():
                        y_arrive(kind, c, d)

        for i in range(ch):
            h = c * ch + i
            ends = []
            for kind in range(2):
                total = zin[kind, h]
                for d in range(1, ys):
                    other = lax.rem(y + d, ys)
                    used = jnp.logical_not(later(kind, other)) | ((c >= raw) & (hops[kind] > 0))
                    total = total + jnp.where(used, slots[kind, other, h], 0.0)
                ends.append(total)
            fwd, bwd = [ends[0]], [ends[1]]
            for b in range(blocks - 1):
                fwd.append(fwd[-1] + terms[0, b, h])
                bwd.insert(0, bwd[0] + terms[1, blocks - 1 - b, h])
            for b in range(blocks):
                at = (toks(b), lanes(h))
                kb, vb, gb = k_ref[at], v_ref[at], d_ref[at]
                fs, bs = fwd[b].astype(BF16), bwd[b].astype(BF16)
                qg_out[at] = ((acc_q[at] + dot(gb, fs, 1, 1)) * factor).astype(BF16)
                kg_out[at] = ((acc_k[at] + dot(vb, bs, 1, 1)) * factor).astype(BF16)
                vg_out[at] = ((acc_v[at] + dot(kb, bs, 1, 0)) * factor).astype(BF16)

    last = jnp.maximum(
        jnp.where(hops[0] > 0, hops[0] * HOP, 0), jnp.where(hops[1] > 0, hops[1] * HOP + LAG, 0)
    )
    edge = (hops[0] == 0) | (hops[1] == 0)

    def turn(t, carry):
        step(0, t - start(0))
        step(1, t - start(1))

        @pl.when(t - EARLY < n)
        def _():
            local(t - EARLY)

        place = t - last

        @pl.when((place >= n - raw) & (place < n))
        def _():
            finish(lax.rem(place + raw, n))

        settled = place - SETTLE

        @pl.when(edge & (settled >= 0) & (settled < n - raw))
        def _():
            finish(settled + raw)

        return carry

    lax.fori_loop(EARLY, steps + SETTLE, turn, 0)

    @pl.when(jnp.logical_not(edge))
    def _():
        lax.fori_loop(raw, n, lambda c, carry: (finish(c), carry)[1], 0)

    for d in range(1, hs):
        sum_copy(mine, d).wait_send()

    def sent(c, carry):
        for kind in range(2):
            for d in range(1, ys):
                other = lax.rem(y + d, ys)

                @pl.when(later(kind, other) | (c < raw) | (hops[kind] > 0))
                def _():
                    y_copy(kind, inc.at[kind], c, d).wait_send()

            @pl.when(hops[kind] < zs - 1)
            def _():
                z_copy(kind, c).wait_send()

        return carry

    lax.fori_loop(0, n, sent, 0)


def store_kernel(a, b, c, a_out, b_out, c_out, sem):
    part = a.shape[0] // STORES
    copies = []
    for i in range(STORES):
        at = slice(i * part, (i + 1) * part)
        for j, (src, dst) in enumerate(((a, a_out), (b, b_out), (c, c_out))):
            copies.append(pltpu.make_async_copy(src.at[at], dst.at[at], sem.at[j, i]))
    for copy in copies:
        copy.start()
    for copy in copies:
        copy.wait()


def shards(sizes, queries, keys, values, attn_out, out_grad, norm_gain):
    seqs, hs = sizes
    zs, ys = split_seq(seqs)
    rows, width = queries.shape
    heads = width // DH
    blocks = rows // GROUP
    ch = 1
    n = heads // ch
    raw = n // 2
    factor = 1.0 / math.sqrt(DH * rows * seqs)
    cfg = (zs, ys, hs, heads, ch, raw, rows, width * hs, factor)
    big = pltpu.VMEM((rows, width), BF16)
    acc = pltpu.VMEM((rows, width), F32)
    state = (heads, DH, DH)
    out = jax.ShapeDtypeStruct((rows, width), BF16)
    dma = pltpu.SemaphoreType.DMA
    flops = 2 * heads * blocks * (6 * GROUP * GROUP * DH + 5 * GROUP * DH * DH)
    held = pl.pallas_call(
        functools.partial(kernel, cfg),
        out_shape=(out, out, out),
        in_specs=[pl.BlockSpec(memory_space=pltpu.HBM)] * 6,
        out_specs=[pl.BlockSpec(memory_space=pltpu.VMEM)] * 3,
        scratch_shapes=[
            big, big, big, big, big,
            pltpu.VMEM((width,), F32),
            acc, acc, acc,
            pltpu.VMEM((2, blocks) + state, F32),
            pltpu.VMEM((2, ys) + state, F32),
            pltpu.VMEM((2,) + state, F32),
            pltpu.VMEM((2,) + state, F32),
            pltpu.VMEM((hs, 8, rows), F32),
            dma((6,)),
            dma((hs - 1,)),
            dma((hs,)),
            dma((2, ys - 1, n)),
            dma((2, ys, n)),
            dma((2, n)),
            dma((2, n)),
        ],
        cost_estimate=pl.CostEstimate(
            flops=flops, bytes_accessed=8 * rows * width * 2, transcendentals=0
        ),
        compiler_params=pltpu.CompilerParams(
            collective_id=0, has_side_effects=True, vmem_limit_bytes=42 * 1024 * 1024
        ),
    )(*[
        pltpu.with_memory_space_constraint(x, pltpu.HBM)
        for x in (queries, keys, values, attn_out, out_grad, norm_gain)
    ])
    return pl.pallas_call(
        store_kernel,
        out_shape=(out, out, out),
        in_specs=[pl.BlockSpec(memory_space=pl.ANY)] * 3,
        out_specs=[pl.BlockSpec(memory_space=pltpu.HBM)] * 3,
        scratch_shapes=[dma((3, STORES))],
        cost_estimate=pl.CostEstimate(
            flops=0, bytes_accessed=3 * rows * width * 2, transcendentals=0
        ),
        compiler_params=pltpu.CompilerParams(vmem_limit_bytes=4 * 1024 * 1024),
    )(*held)


def solution(mesh):
    sizes = (mesh.shape["seq"], mesh.shape["head"])
    spec = P("seq", "head")
    return jax.shard_map(
        functools.partial(shards, sizes),
        mesh=mesh,
        in_specs=(spec,) * 5 + (P("head"),),
        out_specs=(spec,) * 3,
        check_vma=False,
    )
```

```python
import functools
import math

import jax
import jax.numpy as jnp
from jax import lax
from jax.experimental import pallas as pl
from jax.experimental.pallas import tpu as pltpu
from jax.sharding import PartitionSpec as P

DH = 128
GROUP = 256
EPS = 1e-06
MESH = pl.DeviceIdType.MESH
F32 = jnp.float32
BF16 = jnp.bfloat16
LAG = 1
HOP = 2
SETTLE = 3
STORES = 4


def dot(a, b, ca, cb):
    return lax.dot_general(a, b, (((ca,), (cb,)), ((), ())), preferred_element_type=F32)


def split_seq(count):
    inner = 1
    while inner * inner * 4 <= count:
        inner *= 2
    while count % inner:
        inner //= 2
    return count // inner, inner


def kernel(
    cfg,
    q_hbm, k_hbm, v_hbm, o_hbm, d_hbm, gain_hbm,
    qg_out, kg_out, vg_out,
    q_ref, k_ref, v_ref, o_ref, d_ref, gain_ref,
    acc_q, acc_k, acc_v, terms, slots, zin, inc, sums,
    load_sem, sum_send, sum_recv, y_send, y_recv, z_send, z_recv,
):
    zs, ys, hs, heads, ch, raw, rows, full_width, factor = cfg
    n = heads // ch
    blocks = rows // GROUP
    seq = lax.axis_index("seq")
    mine = lax.axis_index("head")
    z = seq // ys
    y = seq % ys
    hops = (z, zs - 1 - z)
    steps = (zs - 1) * HOP + LAG + n

    loads = [
        pltpu.make_async_copy(src, dst, load_sem.at[i])
        for i, (src, dst) in enumerate(
            ((o_hbm, o_ref), (d_hbm, d_ref), (k_hbm, k_ref), (v_hbm, v_ref), (q_hbm, q_ref))
        )
    ]
    for load in loads:
        load.start()
    gain_load = pltpu.make_async_copy(gain_hbm, gain_ref, load_sem.at[5])
    gain_load.start()

    barrier = pltpu.get_barrier_semaphore()

    def greet(s, h):
        pl.semaphore_signal(barrier, inc=1, device_id=(s, h), device_id_type=MESH)

    for d in range(1, hs):
        greet(seq, lax.rem(mine + d, hs))
    for d in range(1, ys):
        greet(z * ys + lax.rem(y + d, ys), mine)

    @pl.when(z > 0)
    def _():
        greet(seq - ys, mine)

    @pl.when(z < zs - 1)
    def _():
        greet(seq + ys, mine)

    for kind in range(2):

        @pl.when(hops[kind] == 0)
        def _():
            zin[kind] = jnp.zeros_like(zin[kind])

    def chunk(c):
        return pl.ds(c * ch, ch)

    def lanes(h):
        return pl.ds(pl.multiple_of(h * DH, DH), DH)

    def toks(b):
        return slice(b * GROUP, (b + 1) * GROUP)

    def y_copy(kind, src, c, d):
        other = lax.rem(y + d, ys)
        return pltpu.make_async_remote_copy(
            src_ref=src.at[chunk(c)],
            dst_ref=slots.at[kind, y, chunk(c)],
            send_sem=y_send.at[kind, d - 1, c],
            recv_sem=y_recv.at[kind, y, c],
            device_id=(z * ys + other, mine),
            device_id_type=MESH,
        )

    def y_arrive(kind, c, d):
        other = lax.rem(y + d, ys)
        pltpu.make_async_remote_copy(
            src_ref=slots.at[kind, other, chunk(c)],
            dst_ref=slots.at[kind, other, chunk(c)],
            send_sem=y_send.at[kind, d - 1, c],
            recv_sem=y_recv.at[kind, other, c],
            device_id=(z * ys + other, mine),
            device_id_type=MESH,
        ).wait_recv()

    def z_copy(kind, c):
        return pltpu.make_async_remote_copy(
            src_ref=inc.at[kind, chunk(c)],
            dst_ref=zin.at[kind, chunk(c)],
            send_sem=z_send.at[kind, c],
            recv_sem=z_recv.at[kind, c],
            device_id=(seq + (ys if kind == 0 else -ys), mine),
            device_id_type=MESH,
        )

    def later(kind, other):
        return other > y if kind == 0 else other < y

    def raw_sent(kind, d):
        return later(kind, lax.rem(y + d, ys)) | (hops[kind] < zs - 1)

    def own_terms(kind, a_ref, b_ref):
        def one(c, carry):
            for i in range(ch):
                h = c * ch + i
                total = None
                for b in range(blocks):
                    part = dot(a_ref[toks(b), lanes(h)], b_ref[toks(b), lanes(h)], 0, 0)
                    terms[kind, b, h] = part
                    total = part if total is None else total + part
                slots[kind, y, h] = total

            @pl.when(c < raw)
            def _():
                for d in range(1, ys):

                    @pl.when(raw_sent(kind, d))
                    def _():
                        y_copy(kind, slots.at[kind, y], c, d).start()

            @pl.when((c >= raw) & (hops[kind] == 0))
            def _():
                step(kind, c - raw, 0)

            return carry

        lax.fori_loop(0, n, one, 0)

    def step(kind, place, first):
        @pl.when((place >= first) & (place < n))
        def _():
            c = lax.rem(place + raw, n)

            @pl.when(hops[kind] > 0)
            def _():
                z_copy(kind, c).wait_recv()

            @pl.when(place >= n - raw)
            def _():
                for d in range(1, ys):
                    other = lax.rem(y + d, ys)

                    @pl.when(jnp.logical_not(later(kind, other)) | (hops[kind] < zs - 1))
                    def _():
                        y_arrive(kind, c, d)

                @pl.when(hops[kind] < zs - 1)
                def _():
                    total = zin[kind, chunk(c)]
                    for s in range(ys):
                        total = total + slots[kind, s, chunk(c)]
                    inc[kind, chunk(c)] = total

            @pl.when(place < n - raw)
            def _():
                inc[kind, chunk(c)] = zin[kind, chunk(c)] + slots[kind, y, chunk(c)]
                for d in range(1, ys):
                    other = lax.rem(y + d, ys)

                    @pl.when(later(kind, other))
                    def _():
                        y_copy(kind, inc.at[kind], c, d).start()

                    @pl.when(jnp.logical_not(later(kind, other)) & (hops[kind] > 0))
                    def _():
                        y_copy(kind, zin.at[kind], c, d).start()

            @pl.when(hops[kind] < zs - 1)
            def _():
                z_copy(kind, c).start()

    def start(kind):
        return hops[kind] * HOP + kind * LAG

    loads[0].wait()
    loads[1].wait()
    gain_load.wait()
    tile = 128
    for r in range(rows // tile):
        rs = slice(r * tile, (r + 1) * tile)

        def partial(h, carry):
            sq, cr = carry
            of = o_ref[rs, lanes(h)].astype(F32)
            sc = gain_ref[lanes(h)][None, :] * d_ref[rs, lanes(h)].astype(F32)
            return sq + of * of, cr + sc * of

        zero = jnp.zeros((tile, DH), F32)
        sq, cr = lax.fori_loop(0, heads, partial, (zero, zero))
        sq = jnp.sum(sq.T, axis=0, keepdims=True)
        cr = jnp.sum(cr.T, axis=0, keepdims=True)
        sums[mine, 0:4, rs] = jnp.broadcast_to(sq, (4, tile))
        sums[mine, 4:8, rs] = jnp.broadcast_to(cr, (4, tile))

    def sum_copy(slot, d):
        return pltpu.make_async_remote_copy(
            src_ref=sums.at[slot],
            dst_ref=sums.at[slot],
            send_sem=sum_send.at[d - 1],
            recv_sem=sum_recv.at[slot],
            device_id=(seq, lax.rem(mine + d, hs)),
            device_id_type=MESH,
        )

    peers = hs - 1 + ys - 1 + jnp.where(z > 0, 1, 0) + jnp.where(z < zs - 1, 1, 0)
    pl.semaphore_wait(barrier, peers)
    for d in range(1, hs):
        sum_copy(mine, d).start()

    loads[2].wait()
    loads[3].wait()
    own_terms(0, k_ref, v_ref)

    for d in range(1, hs):
        sum_copy(lax.rem(mine + d, hs), d).wait_recv()
    total = sums[0]
    for s in range(1, hs):
        total = total + sums[s]
    rms = jnp.sqrt(total[0:1] / full_width + EPS)
    inv_row = 1.0 / rms
    coef_row = total[4:5] / (full_width * (rms * rms * rms))
    for r in range(rows // tile):
        rs = slice(r * tile, (r + 1) * tile)
        inv = jnp.broadcast_to(inv_row[:, rs], (tile, tile)).T
        coef = jnp.broadcast_to(coef_row[:, rs], (tile, tile)).T

        def normed(h, carry):
            of = o_ref[rs, lanes(h)].astype(F32)
            sc = gain_ref[lanes(h)][None, :] * d_ref[rs, lanes(h)].astype(F32)
            d_ref[rs, lanes(h)] = (sc * inv - of * coef).astype(BF16)
            return carry

        lax.fori_loop(0, heads, normed, 0)

    loads[4].wait()
    own_terms(1, q_ref, d_ref)

    def local(c):
        row = lax.broadcasted_iota(jnp.int32, (GROUP, GROUP), 0)
        col = lax.broadcasted_iota(jnp.int32, (GROUP, GROUP), 1)
        for i in range(ch):
            h = c * ch + i
            for b in range(blocks):
                qb = q_ref[toks(b), lanes(h)]
                kb = k_ref[toks(b), lanes(h)]
                vb = v_ref[toks(b), lanes(h)]
                gb = d_ref[toks(b), lanes(h)]
                prods = jnp.where(row >= col, dot(gb, vb, 1, 1), 0.0).astype(BF16)
                acc_q[toks(b), lanes(h)] = dot(prods, kb, 1, 0)
                prods_t = jnp.where(col >= row, dot(vb, gb, 1, 1), 0.0).astype(BF16)
                acc_k[toks(b), lanes(h)] = dot(prods_t, qb, 1, 0)
                scores_t = jnp.where(col >= row, dot(kb, qb, 1, 1), 0.0).astype(BF16)
                acc_v[toks(b), lanes(h)] = dot(scores_t, gb, 1, 0)

    def finish(c):
        @pl.when(c >= raw)
        def _():
            for kind in range(2):
                for d in range(1, ys):
                    other = lax.rem(y + d, ys)

                    @pl.when(jnp.logical_not(later(kind, other)) | (hops[kind] > 0))
                    def _():
                        y_arrive(kind, c, d)

        for i in range(ch):
            h = c * ch + i
            ends = []
            for kind in range(2):
                total = zin[kind, h]
                for d in range(1, ys):
                    other = lax.rem(y + d, ys)
                    used = jnp.logical_not(later(kind, other)) | ((c >= raw) & (hops[kind] > 0))
                    total = total + jnp.where(used, slots[kind, other, h], 0.0)
                ends.append(total)
            fwd, bwd = [ends[0]], [ends[1]]
            for b in range(blocks - 1):
                fwd.append(fwd[-1] + terms[0, b, h])
                bwd.insert(0, bwd[0] + terms[1, blocks - 1 - b, h])
            for b in range(blocks):
                at = (toks(b), lanes(h))
                kb, vb, gb = k_ref[at], v_ref[at], d_ref[at]
                fs, bs = fwd[b].astype(BF16), bwd[b].astype(BF16)
                qg_out[at] = ((acc_q[at] + dot(gb, fs, 1, 1)) * factor).astype(BF16)
                kg_out[at] = ((acc_k[at] + dot(vb, bs, 1, 1)) * factor).astype(BF16)
                vg_out[at] = ((acc_v[at] + dot(kb, bs, 1, 0)) * factor).astype(BF16)

    last = jnp.maximum(start(0), start(1))
    edge = (hops[0] == 0) | (hops[1] == 0)

    def turn(t, carry):
        for kind in range(2):
            step(kind, t - start(kind), jnp.where(hops[kind] == 0, n - raw, 0))

        @pl.when(t < n)
        def _():
            local(t)

        place = t - last

        @pl.when((place >= n - raw) & (place < n))
        def _():
            finish(lax.rem(place + raw, n))

        settled = place - SETTLE

        @pl.when(edge & (settled >= 0) & (settled < n - raw))
        def _():
            finish(settled + raw)

        return carry

    lax.fori_loop(0, steps + SETTLE, turn, 0)

    @pl.when(jnp.logical_not(edge))
    def _():
        lax.fori_loop(raw, n, lambda c, carry: (finish(c), carry)[1], 0)

    for d in range(1, hs):
        sum_copy(mine, d).wait_send()

    def sent(c, carry):
        for kind in range(2):
            for d in range(1, ys):
                other = lax.rem(y + d, ys)

                begun = jnp.where(c < raw, hops[kind] < zs - 1, hops[kind] > 0)

                @pl.when(later(kind, other) | begun)
                def _():
                    y_copy(kind, inc.at[kind], c, d).wait_send()

            @pl.when(hops[kind] < zs - 1)
            def _():
                z_copy(kind, c).wait_send()

        return carry

    lax.fori_loop(0, n, sent, 0)


def store_kernel(a, b, c, a_out, b_out, c_out, sem):
    part = a.shape[0] // STORES
    copies = []
    for i in range(STORES):
        at = slice(i * part, (i + 1) * part)
        for j, (src, dst) in enumerate(((a, a_out), (b, b_out), (c, c_out))):
            copies.append(pltpu.make_async_copy(src.at[at], dst.at[at], sem.at[j, i]))
    for copy in copies:
        copy.start()
    for copy in copies:
        copy.wait()


def shards(sizes, queries, keys, values, attn_out, out_grad, norm_gain):
    seqs, hs = sizes
    zs, ys = split_seq(seqs)
    rows, width = queries.shape
    heads = width // DH
    blocks = rows // GROUP
    ch = 1
    n = heads // ch
    raw = n // 2
    factor = 1.0 / math.sqrt(DH * rows * seqs)
    cfg = (zs, ys, hs, heads, ch, raw, rows, width * hs, factor)
    big = pltpu.VMEM((rows, width), BF16)
    acc = pltpu.VMEM((rows, width), F32)
    state = (heads, DH, DH)
    out = jax.ShapeDtypeStruct((rows, width), BF16)
    dma = pltpu.SemaphoreType.DMA
    flops = 2 * heads * blocks * (6 * GROUP * GROUP * DH + 5 * GROUP * DH * DH)
    held = pl.pallas_call(
        functools.partial(kernel, cfg),
        out_shape=(out, out, out),
        in_specs=[pl.BlockSpec(memory_space=pltpu.HBM)] * 6,
        out_specs=[pl.BlockSpec(memory_space=pltpu.VMEM)] * 3,
        scratch_shapes=[
            big, big, big, big, big,
            pltpu.VMEM((width,), F32),
            acc, acc, acc,
            pltpu.VMEM((2, blocks) + state, F32),
            pltpu.VMEM((2, ys) + state, F32),
            pltpu.VMEM((2,) + state, F32),
            pltpu.VMEM((2,) + state, F32),
            pltpu.VMEM((hs, 8, rows), F32),
            dma((6,)),
            dma((hs - 1,)),
            dma((hs,)),
            dma((2, ys - 1, n)),
            dma((2, ys, n)),
            dma((2, n)),
            dma((2, n)),
        ],
        cost_estimate=pl.CostEstimate(
            flops=flops, bytes_accessed=8 * rows * width * 2, transcendentals=0
        ),
        compiler_params=pltpu.CompilerParams(
            collective_id=0, has_side_effects=True, vmem_limit_bytes=42 * 1024 * 1024
        ),
    )(*[
        pltpu.with_memory_space_constraint(x, pltpu.HBM)
        for x in (queries, keys, values, attn_out, out_grad, norm_gain)
    ])
    return pl.pallas_call(
        store_kernel,
        out_shape=(out, out, out),
        in_specs=[pl.BlockSpec(memory_space=pl.ANY)] * 3,
        out_specs=[pl.BlockSpec(memory_space=pltpu.HBM)] * 3,
        scratch_shapes=[dma((3, STORES))],
        cost_estimate=pl.CostEstimate(
            flops=0, bytes_accessed=3 * rows * width * 2, transcendentals=0
        ),
        compiler_params=pltpu.CompilerParams(vmem_limit_bytes=4 * 1024 * 1024),
    )(*held)


def solution(mesh):
    sizes = (mesh.shape["seq"], mesh.shape["head"])
    spec = P("seq", "head")
    return jax.shard_map(
        functools.partial(shards, sizes),
        mesh=mesh,
        in_specs=(spec,) * 5 + (P("head"),),
        out_specs=(spec,) * 3,
        check_vma=False,
    )
```

```python
import functools
import math

import jax
import jax.numpy as jnp
from jax import lax
from jax.experimental import pallas as pl
from jax.experimental.pallas import tpu as pltpu
from jax.sharding import PartitionSpec as P

DH = 128
GROUP = 256
EPS = 1e-06
MESH = pl.DeviceIdType.MESH
F32 = jnp.float32
BF16 = jnp.bfloat16
LAG = 4
EARLY = 3
HOP = 2
SETTLE = 3
STORES = 4


def dot(a, b, ca, cb):
    return lax.dot_general(a, b, (((ca,), (cb,)), ((), ())), preferred_element_type=F32)


def split_seq(count):
    inner = 1
    while inner * inner * 4 <= count:
        inner *= 2
    while count % inner:
        inner //= 2
    return count // inner, inner


def kernel(
    cfg,
    q_hbm, k_hbm, v_hbm, o_hbm, d_hbm, gain_hbm,
    qg_out, kg_out, vg_out,
    q_ref, k_ref, v_ref, o_ref, d_ref, gain_ref,
    acc_q, acc_k, acc_v, terms, slots, zin, inc, sums,
    load_sem, sum_send, sum_recv, y_send, y_recv, z_send, z_recv,
):
    zs, ys, hs, heads, ch, raw, rows, full_width, factor = cfg
    n = heads // ch
    blocks = rows // GROUP
    seq = lax.axis_index("seq")
    mine = lax.axis_index("head")
    z = seq // ys
    y = seq % ys
    hops = (z, zs - 1 - z)
    steps = (zs - 1) * HOP + LAG + n

    loads = [
        pltpu.make_async_copy(src, dst, load_sem.at[i])
        for i, (src, dst) in enumerate(
            ((k_hbm, k_ref), (v_hbm, v_ref), (o_hbm, o_ref), (d_hbm, d_ref), (q_hbm, q_ref))
        )
    ]
    for load in loads:
        load.start()
    gain_load = pltpu.make_async_copy(gain_hbm, gain_ref, load_sem.at[5])
    gain_load.start()

    barrier = pltpu.get_barrier_semaphore()

    def greet(s, h):
        pl.semaphore_signal(barrier, inc=1, device_id=(s, h), device_id_type=MESH)

    for d in range(1, hs):
        greet(seq, lax.rem(mine + d, hs))
    for d in range(1, ys):
        greet(z * ys + lax.rem(y + d, ys), mine)

    @pl.when(z > 0)
    def _():
        greet(seq - ys, mine)

    @pl.when(z < zs - 1)
    def _():
        greet(seq + ys, mine)

    for kind in range(2):

        @pl.when(hops[kind] == 0)
        def _():
            zin[kind] = jnp.zeros_like(zin[kind])

    def chunk(c):
        return pl.ds(c * ch, ch)

    def lanes(h):
        return pl.ds(pl.multiple_of(h * DH, DH), DH)

    def toks(b):
        return slice(b * GROUP, (b + 1) * GROUP)

    def y_copy(kind, src, c, d):
        other = lax.rem(y + d, ys)
        return pltpu.make_async_remote_copy(
            src_ref=src.at[chunk(c)],
            dst_ref=slots.at[kind, y, chunk(c)],
            send_sem=y_send.at[kind, d - 1, c],
            recv_sem=y_recv.at[kind, y, c],
            device_id=(z * ys + other, mine),
            device_id_type=MESH,
        )

    def y_arrive(kind, c, d):
        other = lax.rem(y + d, ys)
        pltpu.make_async_remote_copy(
            src_ref=slots.at[kind, other, chunk(c)],
            dst_ref=slots.at[kind, other, chunk(c)],
            send_sem=y_send.at[kind, d - 1, c],
            recv_sem=y_recv.at[kind, other, c],
            device_id=(z * ys + other, mine),
            device_id_type=MESH,
        ).wait_recv()

    def z_copy(kind, c):
        return pltpu.make_async_remote_copy(
            src_ref=inc.at[kind, chunk(c)],
            dst_ref=zin.at[kind, chunk(c)],
            send_sem=z_send.at[kind, c],
            recv_sem=z_recv.at[kind, c],
            device_id=(seq + (ys if kind == 0 else -ys), mine),
            device_id_type=MESH,
        )

    def later(kind, other):
        return other > y if kind == 0 else other < y

    def raw_sent(kind, d):
        return later(kind, lax.rem(y + d, ys)) | (hops[kind] < zs - 1)

    def own_terms(kind, a_ref, b_ref):
        def one(c, carry):
            for i in range(ch):
                h = c * ch + i
                total = None
                for b in range(blocks):
                    part = dot(a_ref[toks(b), lanes(h)], b_ref[toks(b), lanes(h)], 0, 0)
                    terms[kind, b, h] = part
                    total = part if total is None else total + part
                slots[kind, y, h] = total

            @pl.when(c < raw)
            def _():
                for d in range(1, ys):

                    @pl.when(raw_sent(kind, d))
                    def _():
                        y_copy(kind, slots.at[kind, y], c, d).start()

            @pl.when((c >= raw) & (hops[kind] == 0))
            def _():
                step(kind, c - raw, 0)

            return carry

        lax.fori_loop(0, n, one, 0)

    def step(kind, place, first):
        @pl.when((place >= first) & (place < n))
        def _():
            c = lax.rem(place + raw, n)

            @pl.when(hops[kind] > 0)
            def _():
                z_copy(kind, c).wait_recv()

            @pl.when(place >= n - raw)
            def _():
                for d in range(1, ys):
                    other = lax.rem(y + d, ys)

                    @pl.when(jnp.logical_not(later(kind, other)) | (hops[kind] < zs - 1))
                    def _():
                        y_arrive(kind, c, d)

                @pl.when(hops[kind] < zs - 1)
                def _():
                    total = zin[kind, chunk(c)]
                    for s in range(ys):
                        total = total + slots[kind, s, chunk(c)]
                    inc[kind, chunk(c)] = total

            @pl.when(place < n - raw)
            def _():
                inc[kind, chunk(c)] = zin[kind, chunk(c)] + slots[kind, y, chunk(c)]
                for d in range(1, ys):
                    other = lax.rem(y + d, ys)

                    @pl.when(later(kind, other))
                    def _():
                        y_copy(kind, inc.at[kind], c, d).start()

                    @pl.when(jnp.logical_not(later(kind, other)) & (hops[kind] > 0))
                    def _():
                        y_copy(kind, zin.at[kind], c, d).start()

            @pl.when(hops[kind] < zs - 1)
            def _():
                z_copy(kind, c).start()

    def start(kind):
        return hops[kind] * HOP + kind * LAG

    loads[0].wait()
    loads[1].wait()
    peers = hs - 1 + ys - 1 + jnp.where(z > 0, 1, 0) + jnp.where(z < zs - 1, 1, 0)
    pl.semaphore_wait(barrier, peers)
    own_terms(0, k_ref, v_ref)

    loads[2].wait()
    loads[3].wait()
    gain_load.wait()
    tile = 128
    for r in range(rows // tile):
        rs = slice(r * tile, (r + 1) * tile)

        def partial(h, carry):
            sq, cr = carry
            of = o_ref[rs, lanes(h)].astype(F32)
            sc = gain_ref[lanes(h)][None, :] * d_ref[rs, lanes(h)].astype(F32)
            return sq + of * of, cr + sc * of

        zero = jnp.zeros((tile, DH), F32)
        sq, cr = lax.fori_loop(0, heads, partial, (zero, zero))
        sq = jnp.sum(sq.T, axis=0, keepdims=True)
        cr = jnp.sum(cr.T, axis=0, keepdims=True)
        sums[mine, 0:4, rs] = jnp.broadcast_to(sq, (4, tile))
        sums[mine, 4:8, rs] = jnp.broadcast_to(cr, (4, tile))

    def sum_copy(slot, d):
        return pltpu.make_async_remote_copy(
            src_ref=sums.at[slot],
            dst_ref=sums.at[slot],
            send_sem=sum_send.at[d - 1],
            recv_sem=sum_recv.at[slot],
            device_id=(seq, lax.rem(mine + d, hs)),
            device_id_type=MESH,
        )

    for d in range(1, hs):
        sum_copy(mine, d).start()
    for t in range(EARLY):
        step(0, t - start(0), jnp.where(z == 0, n - raw, 0))
    for d in range(1, hs):
        sum_copy(lax.rem(mine + d, hs), d).wait_recv()
    total = sums[0]
    for s in range(1, hs):
        total = total + sums[s]
    rms = jnp.sqrt(total[0:1] / full_width + EPS)
    inv_row = 1.0 / rms
    coef_row = total[4:5] / (full_width * (rms * rms * rms))
    for r in range(rows // tile):
        rs = slice(r * tile, (r + 1) * tile)
        inv = jnp.broadcast_to(inv_row[:, rs], (tile, tile)).T
        coef = jnp.broadcast_to(coef_row[:, rs], (tile, tile)).T

        def normed(h, carry):
            of = o_ref[rs, lanes(h)].astype(F32)
            sc = gain_ref[lanes(h)][None, :] * d_ref[rs, lanes(h)].astype(F32)
            d_ref[rs, lanes(h)] = (sc * inv - of * coef).astype(BF16)
            return carry

        lax.fori_loop(0, heads, normed, 0)

    loads[4].wait()
    own_terms(1, q_ref, d_ref)

    def local(c):
        row = lax.broadcasted_iota(jnp.int32, (GROUP, GROUP), 0)
        col = lax.broadcasted_iota(jnp.int32, (GROUP, GROUP), 1)
        for i in range(ch):
            h = c * ch + i
            for b in range(blocks):
                qb = q_ref[toks(b), lanes(h)]
                kb = k_ref[toks(b), lanes(h)]
                vb = v_ref[toks(b), lanes(h)]
                gb = d_ref[toks(b), lanes(h)]
                prods = jnp.where(row >= col, dot(gb, vb, 1, 1), 0.0).astype(BF16)
                acc_q[toks(b), lanes(h)] = dot(prods, kb, 1, 0)
                prods_t = jnp.where(col >= row, dot(vb, gb, 1, 1), 0.0).astype(BF16)
                acc_k[toks(b), lanes(h)] = dot(prods_t, qb, 1, 0)
                scores_t = jnp.where(col >= row, dot(kb, qb, 1, 1), 0.0).astype(BF16)
                acc_v[toks(b), lanes(h)] = dot(scores_t, gb, 1, 0)

    def finish(c):
        @pl.when(c >= raw)
        def _():
            for kind in range(2):
                for d in range(1, ys):
                    other = lax.rem(y + d, ys)

                    @pl.when(jnp.logical_not(later(kind, other)) | (hops[kind] > 0))
                    def _():
                        y_arrive(kind, c, d)

        for i in range(ch):
            h = c * ch + i
            ends = []
            for kind in range(2):
                total = zin[kind, h]
                for d in range(1, ys):
                    other = lax.rem(y + d, ys)
                    used = jnp.logical_not(later(kind, other)) | ((c >= raw) & (hops[kind] > 0))
                    total = total + jnp.where(used, slots[kind, other, h], 0.0)
                ends.append(total)
            fwd, bwd = [ends[0]], [ends[1]]
            for b in range(blocks - 1):
                fwd.append(fwd[-1] + terms[0, b, h])
                bwd.insert(0, bwd[0] + terms[1, blocks - 1 - b, h])
            for b in range(blocks):
                at = (toks(b), lanes(h))
                kb, vb, gb = k_ref[at], v_ref[at], d_ref[at]
                fs, bs = fwd[b].astype(BF16), bwd[b].astype(BF16)
                qg_out[at] = ((acc_q[at] + dot(gb, fs, 1, 1)) * factor).astype(BF16)
                kg_out[at] = ((acc_k[at] + dot(vb, bs, 1, 1)) * factor).astype(BF16)
                vg_out[at] = ((acc_v[at] + dot(kb, bs, 1, 0)) * factor).astype(BF16)

    last = jnp.maximum(start(0), start(1))
    edge = (hops[0] == 0) | (hops[1] == 0)

    def turn(t, carry):
        for kind in range(2):
            step(kind, t - start(kind), jnp.where(hops[kind] == 0, n - raw, 0))

        @pl.when(t - EARLY < n)
        def _():
            local(t - EARLY)

        place = t - last

        @pl.when((place >= n - raw) & (place < n))
        def _():
            finish(lax.rem(place + raw, n))

        settled = place - SETTLE

        @pl.when(edge & (settled >= 0) & (settled < n - raw))
        def _():
            finish(settled + raw)

        return carry

    lax.fori_loop(EARLY, steps + SETTLE, turn, 0)

    @pl.when(jnp.logical_not(edge))
    def _():
        lax.fori_loop(raw, n, lambda c, carry: (finish(c), carry)[1], 0)

    for d in range(1, hs):
        sum_copy(mine, d).wait_send()

    def sent(c, carry):
        for kind in range(2):
            for d in range(1, ys):
                other = lax.rem(y + d, ys)

                begun = jnp.where(c < raw, hops[kind] < zs - 1, hops[kind] > 0)

                @pl.when(later(kind, other) | begun)
                def _():
                    y_copy(kind, inc.at[kind], c, d).wait_send()

            @pl.when(hops[kind] < zs - 1)
            def _():
                z_copy(kind, c).wait_send()

        return carry

    lax.fori_loop(0, n, sent, 0)


def store_kernel(a, b, c, a_out, b_out, c_out, sem):
    part = a.shape[0] // STORES
    copies = []
    for i in range(STORES):
        at = slice(i * part, (i + 1) * part)
        for j, (src, dst) in enumerate(((a, a_out), (b, b_out), (c, c_out))):
            copies.append(pltpu.make_async_copy(src.at[at], dst.at[at], sem.at[j, i]))
    for copy in copies:
        copy.start()
    for copy in copies:
        copy.wait()


def shards(sizes, queries, keys, values, attn_out, out_grad, norm_gain):
    seqs, hs = sizes
    zs, ys = split_seq(seqs)
    rows, width = queries.shape
    heads = width // DH
    blocks = rows // GROUP
    ch = 1
    n = heads // ch
    raw = n // 2
    factor = 1.0 / math.sqrt(DH * rows * seqs)
    cfg = (zs, ys, hs, heads, ch, raw, rows, width * hs, factor)
    big = pltpu.VMEM((rows, width), BF16)
    acc = pltpu.VMEM((rows, width), F32)
    state = (heads, DH, DH)
    out = jax.ShapeDtypeStruct((rows, width), BF16)
    dma = pltpu.SemaphoreType.DMA
    flops = 2 * heads * blocks * (6 * GROUP * GROUP * DH + 5 * GROUP * DH * DH)
    held = pl.pallas_call(
        functools.partial(kernel, cfg),
        out_shape=(out, out, out),
        in_specs=[pl.BlockSpec(memory_space=pltpu.HBM)] * 6,
        out_specs=[pl.BlockSpec(memory_space=pltpu.VMEM)] * 3,
        scratch_shapes=[
            big, big, big, big, big,
            pltpu.VMEM((width,), F32),
            acc, acc, acc,
            pltpu.VMEM((2, blocks) + state, F32),
            pltpu.VMEM((2, ys) + state, F32),
            pltpu.VMEM((2,) + state, F32),
            pltpu.VMEM((2,) + state, F32),
            pltpu.VMEM((hs, 8, rows), F32),
            dma((6,)),
            dma((hs - 1,)),
            dma((hs,)),
            dma((2, ys - 1, n)),
            dma((2, ys, n)),
            dma((2, n)),
            dma((2, n)),
        ],
        cost_estimate=pl.CostEstimate(
            flops=flops, bytes_accessed=8 * rows * width * 2, transcendentals=0
        ),
        compiler_params=pltpu.CompilerParams(
            collective_id=0, has_side_effects=True, vmem_limit_bytes=42 * 1024 * 1024
        ),
    )(*[
        pltpu.with_memory_space_constraint(x, pltpu.HBM)
        for x in (queries, keys, values, attn_out, out_grad, norm_gain)
    ])
    return pl.pallas_call(
        store_kernel,
        out_shape=(out, out, out),
        in_specs=[pl.BlockSpec(memory_space=pl.ANY)] * 3,
        out_specs=[pl.BlockSpec(memory_space=pltpu.HBM)] * 3,
        scratch_shapes=[dma((3, STORES))],
        cost_estimate=pl.CostEstimate(
            flops=0, bytes_accessed=3 * rows * width * 2, transcendentals=0
        ),
        compiler_params=pltpu.CompilerParams(vmem_limit_bytes=4 * 1024 * 1024),
    )(*held)


def solution(mesh):
    sizes = (mesh.shape["seq"], mesh.shape["head"])
    spec = P("seq", "head")
    return jax.shard_map(
        functools.partial(shards, sizes),
        mesh=mesh,
        in_specs=(spec,) * 5 + (P("head"),),
        out_specs=(spec,) * 3,
        check_vma=False,
    )
```

```python
import functools
import math

import jax
import jax.numpy as jnp
from jax import lax
from jax.experimental import pallas as pl
from jax.experimental.pallas import tpu as pltpu
from jax.sharding import PartitionSpec as P

DH = 128
GROUP = 256
EPS = 1e-06
MESH = pl.DeviceIdType.MESH
F32 = jnp.float32
BF16 = jnp.bfloat16
LAG = 6
EARLY = 5
HOP = 3
SETTLE = 3
STORES = 4


def dot(a, b, ca, cb):
    return lax.dot_general(a, b, (((ca,), (cb,)), ((), ())), preferred_element_type=F32)


def split_seq(count):
    inner = 1
    while inner * inner * 4 <= count:
        inner *= 2
    while count % inner:
        inner //= 2
    return count // inner, inner


def kernel(
    cfg,
    q_hbm, k_hbm, v_hbm, o_hbm, d_hbm, gain_hbm,
    qg_out, kg_out, vg_out,
    q_ref, k_ref, v_ref, o_ref, d_ref, gain_ref,
    acc_q, acc_k, acc_v, terms, slots, zin, inc, sums,
    load_sem, sum_send, sum_recv, y_send, y_recv, z_send, z_recv,
):
    zs, ys, hs, heads, ch, raw, rows, full_width, factor = cfg
    n = heads // ch
    blocks = rows // GROUP
    seq = lax.axis_index("seq")
    mine = lax.axis_index("head")
    z = seq // ys
    y = seq % ys
    hops = (z, zs - 1 - z)
    steps = (zs - 1) * HOP + LAG + n

    loads = [
        pltpu.make_async_copy(src, dst, load_sem.at[i])
        for i, (src, dst) in enumerate(
            ((k_hbm, k_ref), (v_hbm, v_ref), (o_hbm, o_ref), (d_hbm, d_ref), (q_hbm, q_ref))
        )
    ]
    for load in loads:
        load.start()
    gain_load = pltpu.make_async_copy(gain_hbm, gain_ref, load_sem.at[5])
    gain_load.start()

    barrier = pltpu.get_barrier_semaphore()

    def greet(s, h):
        pl.semaphore_signal(barrier, inc=1, device_id=(s, h), device_id_type=MESH)

    for d in range(1, hs):
        greet(seq, lax.rem(mine + d, hs))
    for d in range(1, ys):
        greet(z * ys + lax.rem(y + d, ys), mine)

    @pl.when(z > 0)
    def _():
        greet(seq - ys, mine)

    @pl.when(z < zs - 1)
    def _():
        greet(seq + ys, mine)

    for kind in range(2):

        @pl.when(hops[kind] == 0)
        def _():
            zin[kind] = jnp.zeros_like(zin[kind])

    def chunk(c):
        return pl.ds(c * ch, ch)

    def lanes(h):
        return pl.ds(pl.multiple_of(h * DH, DH), DH)

    def toks(b):
        return slice(b * GROUP, (b + 1) * GROUP)

    def y_copy(kind, src, c, d):
        other = lax.rem(y + d, ys)
        return pltpu.make_async_remote_copy(
            src_ref=src.at[chunk(c)],
            dst_ref=slots.at[kind, y, chunk(c)],
            send_sem=y_send.at[kind, d - 1, c],
            recv_sem=y_recv.at[kind, y, c],
            device_id=(z * ys + other, mine),
            device_id_type=MESH,
        )

    def y_arrive(kind, c, d):
        other = lax.rem(y + d, ys)
        pltpu.make_async_remote_copy(
            src_ref=slots.at[kind, other, chunk(c)],
            dst_ref=slots.at[kind, other, chunk(c)],
            send_sem=y_send.at[kind, d - 1, c],
            recv_sem=y_recv.at[kind, other, c],
            device_id=(z * ys + other, mine),
            device_id_type=MESH,
        ).wait_recv()

    def z_copy(kind, c):
        return pltpu.make_async_remote_copy(
            src_ref=inc.at[kind, chunk(c)],
            dst_ref=zin.at[kind, chunk(c)],
            send_sem=z_send.at[kind, c],
            recv_sem=z_recv.at[kind, c],
            device_id=(seq + (ys if kind == 0 else -ys), mine),
            device_id_type=MESH,
        )

    def later(kind, other):
        return other > y if kind == 0 else other < y

    def raw_sent(kind, d):
        return later(kind, lax.rem(y + d, ys)) | (hops[kind] < zs - 1)

    def own_terms(kind, a_ref, b_ref):
        def one(c, carry):
            for i in range(ch):
                h = c * ch + i
                total = None
                for b in range(blocks):
                    part = dot(a_ref[toks(b), lanes(h)], b_ref[toks(b), lanes(h)], 0, 0)
                    terms[kind, b, h] = part
                    total = part if total is None else total + part
                slots[kind, y, h] = total

            @pl.when(c < raw)
            def _():
                for d in range(1, ys):

                    @pl.when(raw_sent(kind, d))
                    def _():
                        y_copy(kind, slots.at[kind, y], c, d).start()

            @pl.when((c >= raw) & (hops[kind] == 0))
            def _():
                step(kind, c - raw, 0)

            return carry

        lax.fori_loop(0, n, one, 0)

    def step(kind, place, first):
        @pl.when((place >= first) & (place < n))
        def _():
            c = lax.rem(place + raw, n)

            @pl.when(hops[kind] > 0)
            def _():
                z_copy(kind, c).wait_recv()

            @pl.when(place >= n - raw)
            def _():
                for d in range(1, ys):
                    other = lax.rem(y + d, ys)

                    @pl.when(jnp.logical_not(later(kind, other)) | (hops[kind] < zs - 1))
                    def _():
                        y_arrive(kind, c, d)

                @pl.when(hops[kind] < zs - 1)
                def _():
                    total = zin[kind, chunk(c)]
                    for s in range(ys):
                        total = total + slots[kind, s, chunk(c)]
                    inc[kind, chunk(c)] = total

            @pl.when(place < n - raw)
            def _():
                inc[kind, chunk(c)] = zin[kind, chunk(c)] + slots[kind, y, chunk(c)]
                for d in range(1, ys):
                    other = lax.rem(y + d, ys)

                    @pl.when(later(kind, other))
                    def _():
                        y_copy(kind, inc.at[kind], c, d).start()

                    @pl.when(jnp.logical_not(later(kind, other)) & (hops[kind] > 0))
                    def _():
                        y_copy(kind, zin.at[kind], c, d).start()

            @pl.when(hops[kind] < zs - 1)
            def _():
                z_copy(kind, c).start()

    def start(kind):
        return jnp.where(hops[kind] == 0, EARLY - n + raw, hops[kind] * HOP + kind * LAG)

    loads[0].wait()
    loads[1].wait()
    peers = hs - 1 + ys - 1 + jnp.where(z > 0, 1, 0) + jnp.where(z < zs - 1, 1, 0)
    pl.semaphore_wait(barrier, peers)
    own_terms(0, k_ref, v_ref)

    loads[2].wait()
    loads[3].wait()
    gain_load.wait()
    tile = 128
    for r in range(rows // tile):
        rs = slice(r * tile, (r + 1) * tile)

        def partial(h, carry):
            sq, cr = carry
            of = o_ref[rs, lanes(h)].astype(F32)
            sc = gain_ref[lanes(h)][None, :] * d_ref[rs, lanes(h)].astype(F32)
            return sq + of * of, cr + sc * of

        zero = jnp.zeros((tile, DH), F32)
        sq, cr = lax.fori_loop(0, heads, partial, (zero, zero))
        sq = jnp.sum(sq.T, axis=0, keepdims=True)
        cr = jnp.sum(cr.T, axis=0, keepdims=True)
        sums[mine, 0:4, rs] = jnp.broadcast_to(sq, (4, tile))
        sums[mine, 4:8, rs] = jnp.broadcast_to(cr, (4, tile))

    def sum_copy(slot, d):
        return pltpu.make_async_remote_copy(
            src_ref=sums.at[slot],
            dst_ref=sums.at[slot],
            send_sem=sum_send.at[d - 1],
            recv_sem=sum_recv.at[slot],
            device_id=(seq, lax.rem(mine + d, hs)),
            device_id_type=MESH,
        )

    for d in range(1, hs):
        sum_copy(mine, d).start()
    for t in range(EARLY):
        step(0, t - start(0), jnp.where(z == 0, n - raw, 0))
    for d in range(1, hs):
        sum_copy(lax.rem(mine + d, hs), d).wait_recv()
    total = sums[0]
    for s in range(1, hs):
        total = total + sums[s]
    rms = jnp.sqrt(total[0:1] / full_width + EPS)
    inv_row = 1.0 / rms
    coef_row = total[4:5] / (full_width * (rms * rms * rms))
    for r in range(rows // tile):
        rs = slice(r * tile, (r + 1) * tile)
        inv = jnp.broadcast_to(inv_row[:, rs], (tile, tile)).T
        coef = jnp.broadcast_to(coef_row[:, rs], (tile, tile)).T

        def normed(h, carry):
            of = o_ref[rs, lanes(h)].astype(F32)
            sc = gain_ref[lanes(h)][None, :] * d_ref[rs, lanes(h)].astype(F32)
            d_ref[rs, lanes(h)] = (sc * inv - of * coef).astype(BF16)
            return carry

        lax.fori_loop(0, heads, normed, 0)

    loads[4].wait()
    own_terms(1, q_ref, d_ref)

    def local(c):
        row = lax.broadcasted_iota(jnp.int32, (GROUP, GROUP), 0)
        col = lax.broadcasted_iota(jnp.int32, (GROUP, GROUP), 1)
        for i in range(ch):
            h = c * ch + i
            for b in range(blocks):
                qb = q_ref[toks(b), lanes(h)]
                kb = k_ref[toks(b), lanes(h)]
                vb = v_ref[toks(b), lanes(h)]
                gb = d_ref[toks(b), lanes(h)]
                prods = jnp.where(row >= col, dot(gb, vb, 1, 1), 0.0).astype(BF16)
                acc_q[toks(b), lanes(h)] = dot(prods, kb, 1, 0)
                prods_t = jnp.where(col >= row, dot(vb, gb, 1, 1), 0.0).astype(BF16)
                acc_k[toks(b), lanes(h)] = dot(prods_t, qb, 1, 0)
                scores_t = jnp.where(col >= row, dot(kb, qb, 1, 1), 0.0).astype(BF16)
                acc_v[toks(b), lanes(h)] = dot(scores_t, gb, 1, 0)

    def finish(c):
        @pl.when(c >= raw)
        def _():
            for kind in range(2):
                for d in range(1, ys):
                    other = lax.rem(y + d, ys)

                    @pl.when(jnp.logical_not(later(kind, other)) | (hops[kind] > 0))
                    def _():
                        y_arrive(kind, c, d)

        for i in range(ch):
            h = c * ch + i
            ends = []
            for kind in range(2):
                total = zin[kind, h]
                for d in range(1, ys):
                    other = lax.rem(y + d, ys)
                    used = jnp.logical_not(later(kind, other)) | ((c >= raw) & (hops[kind] > 0))
                    total = total + jnp.where(used, slots[kind, other, h], 0.0)
                ends.append(total)
            fwd, bwd = [ends[0]], [ends[1]]
            for b in range(blocks - 1):
                fwd.append(fwd[-1] + terms[0, b, h])
                bwd.insert(0, bwd[0] + terms[1, blocks - 1 - b, h])
            for b in range(blocks):
                at = (toks(b), lanes(h))
                kb, vb, gb = k_ref[at], v_ref[at], d_ref[at]
                fs, bs = fwd[b].astype(BF16), bwd[b].astype(BF16)
                qg_out[at] = ((acc_q[at] + dot(gb, fs, 1, 1)) * factor).astype(BF16)
                kg_out[at] = ((acc_k[at] + dot(vb, bs, 1, 1)) * factor).astype(BF16)
                vg_out[at] = ((acc_v[at] + dot(kb, bs, 1, 0)) * factor).astype(BF16)

    last = jnp.maximum(start(0), start(1))
    edge = (hops[0] == 0) | (hops[1] == 0)

    def turn(t, carry):
        for kind in range(2):
            step(kind, t - start(kind), jnp.where(hops[kind] == 0, n - raw, 0))

        @pl.when(t - EARLY < n)
        def _():
            local(t - EARLY)

        place = t - last

        @pl.when((place >= n - raw) & (place < n))
        def _():
            finish(lax.rem(place + raw, n))

        settled = place - SETTLE

        @pl.when(edge & (settled >= 0) & (settled < n - raw))
        def _():
            finish(settled + raw)

        return carry

    lax.fori_loop(EARLY, steps + SETTLE, turn, 0)

    @pl.when(jnp.logical_not(edge))
    def _():
        lax.fori_loop(raw, n, lambda c, carry: (finish(c), carry)[1], 0)

    for d in range(1, hs):
        sum_copy(mine, d).wait_send()

    def sent(c, carry):
        for kind in range(2):
            for d in range(1, ys):
                other = lax.rem(y + d, ys)

                begun = jnp.where(c < raw, hops[kind] < zs - 1, hops[kind] > 0)

                @pl.when(later(kind, other) | begun)
                def _():
                    y_copy(kind, inc.at[kind], c, d).wait_send()

            @pl.when(hops[kind] < zs - 1)
            def _():
                z_copy(kind, c).wait_send()

        return carry

    lax.fori_loop(0, n, sent, 0)


def store_kernel(a, b, c, a_out, b_out, c_out, sem):
    part = a.shape[0] // STORES
    copies = []
    for i in range(STORES):
        at = slice(i * part, (i + 1) * part)
        for j, (src, dst) in enumerate(((a, a_out), (b, b_out), (c, c_out))):
            copies.append(pltpu.make_async_copy(src.at[at], dst.at[at], sem.at[j, i]))
    for copy in copies:
        copy.start()
    for copy in copies:
        copy.wait()


def shards(sizes, queries, keys, values, attn_out, out_grad, norm_gain):
    seqs, hs = sizes
    zs, ys = split_seq(seqs)
    rows, width = queries.shape
    heads = width // DH
    blocks = rows // GROUP
    ch = 1
    n = heads // ch
    raw = n // 2
    factor = 1.0 / math.sqrt(DH * rows * seqs)
    cfg = (zs, ys, hs, heads, ch, raw, rows, width * hs, factor)
    big = pltpu.VMEM((rows, width), BF16)
    acc = pltpu.VMEM((rows, width), F32)
    state = (heads, DH, DH)
    out = jax.ShapeDtypeStruct((rows, width), BF16)
    dma = pltpu.SemaphoreType.DMA
    flops = 2 * heads * blocks * (6 * GROUP * GROUP * DH + 5 * GROUP * DH * DH)
    held = pl.pallas_call(
        functools.partial(kernel, cfg),
        out_shape=(out, out, out),
        in_specs=[pl.BlockSpec(memory_space=pltpu.HBM)] * 6,
        out_specs=[pl.BlockSpec(memory_space=pltpu.VMEM)] * 3,
        scratch_shapes=[
            big, big, big, big, big,
            pltpu.VMEM((width,), F32),
            acc, acc, acc,
            pltpu.VMEM((2, blocks) + state, F32),
            pltpu.VMEM((2, ys) + state, F32),
            pltpu.VMEM((2,) + state, F32),
            pltpu.VMEM((2,) + state, F32),
            pltpu.VMEM((hs, 8, rows), F32),
            dma((6,)),
            dma((hs - 1,)),
            dma((hs,)),
            dma((2, ys - 1, n)),
            dma((2, ys, n)),
            dma((2, n)),
            dma((2, n)),
        ],
        cost_estimate=pl.CostEstimate(
            flops=flops, bytes_accessed=8 * rows * width * 2, transcendentals=0
        ),
        compiler_params=pltpu.CompilerParams(
            collective_id=0, has_side_effects=True, vmem_limit_bytes=42 * 1024 * 1024
        ),
    )(*[
        pltpu.with_memory_space_constraint(x, pltpu.HBM)
        for x in (queries, keys, values, attn_out, out_grad, norm_gain)
    ])
    return pl.pallas_call(
        store_kernel,
        out_shape=(out, out, out),
        in_specs=[pl.BlockSpec(memory_space=pl.ANY)] * 3,
        out_specs=[pl.BlockSpec(memory_space=pltpu.HBM)] * 3,
        scratch_shapes=[dma((3, STORES))],
        cost_estimate=pl.CostEstimate(
            flops=0, bytes_accessed=3 * rows * width * 2, transcendentals=0
        ),
        compiler_params=pltpu.CompilerParams(vmem_limit_bytes=4 * 1024 * 1024),
    )(*held)


def solution(mesh):
    sizes = (mesh.shape["seq"], mesh.shape["head"])
    spec = P("seq", "head")
    return jax.shard_map(
        functools.partial(shards, sizes),
        mesh=mesh,
        in_specs=(spec,) * 5 + (P("head"),),
        out_specs=(spec,) * 3,
        check_vma=False,
    )
```

```python
import functools
import math

import jax
import jax.numpy as jnp
from jax import lax
from jax.experimental import pallas as pl
from jax.experimental.pallas import tpu as pltpu
from jax.sharding import PartitionSpec as P

DH = 128
GROUP = 256
EPS = 1e-06
MESH = pl.DeviceIdType.MESH
F32 = jnp.float32
BF16 = jnp.bfloat16
LAG = 6
EARLY = 5
HOP = 3
SETTLE = 3
STORES = 4


def dot(a, b, ca, cb):
    return lax.dot_general(a, b, (((ca,), (cb,)), ((), ())), preferred_element_type=F32)


def split_seq(count):
    inner = 1
    while inner * inner * 4 <= count:
        inner *= 2
    while count % inner:
        inner //= 2
    return count // inner, inner


def kernel(
    cfg,
    q_hbm, k_hbm, v_hbm, o_hbm, d_hbm, gain_hbm,
    qg_out, kg_out, vg_out,
    q_ref, k_ref, v_ref, o_ref, d_ref, gain_ref,
    acc_q, acc_k, acc_v, terms, slots, zin, inc, sums,
    load_sem, sum_send, sum_recv, y_send, y_recv, z_send, z_recv,
):
    zs, ys, hs, heads, ch, raw, rows, full_width, factor = cfg
    n = heads // ch
    blocks = rows // GROUP
    seq = lax.axis_index("seq")
    mine = lax.axis_index("head")
    z = seq // ys
    y = seq % ys
    hops = (z, zs - 1 - z)
    steps = (zs - 1) * HOP + LAG + n

    loads = [
        pltpu.make_async_copy(src, dst, load_sem.at[i])
        for i, (src, dst) in enumerate(
            ((k_hbm, k_ref), (v_hbm, v_ref), (o_hbm, o_ref), (d_hbm, d_ref), (q_hbm, q_ref))
        )
    ]
    for load in loads:
        load.start()
    gain_load = pltpu.make_async_copy(gain_hbm, gain_ref, load_sem.at[5])
    gain_load.start()

    barrier = pltpu.get_barrier_semaphore()

    def greet(s, h):
        pl.semaphore_signal(barrier, inc=1, device_id=(s, h), device_id_type=MESH)

    for d in range(1, hs):
        greet(seq, lax.rem(mine + d, hs))
    for d in range(1, ys):
        greet(z * ys + lax.rem(y + d, ys), mine)

    @pl.when(z > 0)
    def _():
        greet(seq - ys, mine)

    @pl.when(z < zs - 1)
    def _():
        greet(seq + ys, mine)

    for kind in range(2):

        @pl.when(hops[kind] == 0)
        def _():
            zin[kind] = jnp.zeros_like(zin[kind])

    def chunk(c):
        return pl.ds(c * ch, ch)

    def lanes(h):
        return pl.ds(pl.multiple_of(h * DH, DH), DH)

    def toks(b):
        return slice(b * GROUP, (b + 1) * GROUP)

    def y_copy(kind, src, c, d):
        other = lax.rem(y + d, ys)
        return pltpu.make_async_remote_copy(
            src_ref=src.at[chunk(c)],
            dst_ref=slots.at[kind, y, chunk(c)],
            send_sem=y_send.at[kind, d - 1, c],
            recv_sem=y_recv.at[kind, y, c],
            device_id=(z * ys + other, mine),
            device_id_type=MESH,
        )

    def y_arrive(kind, c, d):
        other = lax.rem(y + d, ys)
        pltpu.make_async_remote_copy(
            src_ref=slots.at[kind, other, chunk(c)],
            dst_ref=slots.at[kind, other, chunk(c)],
            send_sem=y_send.at[kind, d - 1, c],
            recv_sem=y_recv.at[kind, other, c],
            device_id=(z * ys + other, mine),
            device_id_type=MESH,
        ).wait_recv()

    def z_copy(kind, c):
        return pltpu.make_async_remote_copy(
            src_ref=inc.at[kind, chunk(c)],
            dst_ref=zin.at[kind, chunk(c)],
            send_sem=z_send.at[kind, c],
            recv_sem=z_recv.at[kind, c],
            device_id=(seq + (ys if kind == 0 else -ys), mine),
            device_id_type=MESH,
        )

    def later(kind, other):
        return other > y if kind == 0 else other < y

    def raw_sent(kind, d):
        return later(kind, lax.rem(y + d, ys)) | (hops[kind] < zs - 1)

    def own_terms(kind, a_ref, b_ref):
        def one(c, carry):
            for i in range(ch):
                h = c * ch + i
                total = None
                for b in range(blocks):
                    part = dot(a_ref[toks(b), lanes(h)], b_ref[toks(b), lanes(h)], 0, 0)
                    terms[kind, b, h] = part
                    total = part if total is None else total + part
                slots[kind, y, h] = total

            @pl.when(c < raw)
            def _():
                for d in range(1, ys):

                    @pl.when(raw_sent(kind, d))
                    def _():
                        y_copy(kind, slots.at[kind, y], c, d).start()

            @pl.when((c >= raw) & (hops[kind] == 0))
            def _():
                step(kind, c - raw, 0)

            return carry

        lax.fori_loop(0, n, one, 0)

    def step(kind, place, first):
        @pl.when((place >= first) & (place < n))
        def _():
            c = lax.rem(place + raw, n)

            @pl.when(hops[kind] > 0)
            def _():
                z_copy(kind, c).wait_recv()

            @pl.when(place >= n - raw)
            def _():
                for d in range(1, ys):
                    other = lax.rem(y + d, ys)

                    @pl.when(jnp.logical_not(later(kind, other)) | (hops[kind] < zs - 1))
                    def _():
                        y_arrive(kind, c, d)

                @pl.when(hops[kind] < zs - 1)
                def _():
                    total = zin[kind, chunk(c)]
                    for s in range(ys):
                        total = total + slots[kind, s, chunk(c)]
                    inc[kind, chunk(c)] = total

            @pl.when(place < n - raw)
            def _():
                inc[kind, chunk(c)] = zin[kind, chunk(c)] + slots[kind, y, chunk(c)]
                for d in range(1, ys):
                    other = lax.rem(y + d, ys)

                    @pl.when(later(kind, other))
                    def _():
                        y_copy(kind, inc.at[kind], c, d).start()

                    @pl.when(jnp.logical_not(later(kind, other)) & (hops[kind] > 0))
                    def _():
                        y_copy(kind, zin.at[kind], c, d).start()

            @pl.when(hops[kind] < zs - 1)
            def _():
                z_copy(kind, c).start()

    def start(kind):
        return jnp.where(hops[kind] == 0, EARLY - n + raw, hops[kind] * HOP + kind * LAG)

    loads[0].wait()
    loads[1].wait()
    peers = hs - 1 + ys - 1 + jnp.where(z > 0, 1, 0) + jnp.where(z < zs - 1, 1, 0)
    pl.semaphore_wait(barrier, peers)
    own_terms(0, k_ref, v_ref)

    loads[2].wait()
    loads[3].wait()
    gain_load.wait()
    tile = 128
    for r in range(rows // tile):
        rs = slice(r * tile, (r + 1) * tile)

        def partial(h, carry):
            sq, cr = carry
            of = o_ref[rs, lanes(h)].astype(F32)
            sc = gain_ref[lanes(h)][None, :] * d_ref[rs, lanes(h)].astype(F32)
            return sq + of * of, cr + sc * of

        zero = jnp.zeros((tile, DH), F32)
        sq, cr = lax.fori_loop(0, heads, partial, (zero, zero))
        sq = jnp.sum(sq.T, axis=0, keepdims=True)
        cr = jnp.sum(cr.T, axis=0, keepdims=True)
        sums[mine, 0:4, rs] = jnp.broadcast_to(sq, (4, tile))
        sums[mine, 4:8, rs] = jnp.broadcast_to(cr, (4, tile))

    def sum_copy(slot, d):
        return pltpu.make_async_remote_copy(
            src_ref=sums.at[slot],
            dst_ref=sums.at[slot],
            send_sem=sum_send.at[d - 1],
            recv_sem=sum_recv.at[slot],
            device_id=(seq, lax.rem(mine + d, hs)),
            device_id_type=MESH,
        )

    for d in range(1, hs):
        sum_copy(mine, d).start()
    for t in range(EARLY):
        step(0, t - start(0), jnp.where(z == 0, n - raw, 0))
    for d in range(1, hs):
        sum_copy(lax.rem(mine + d, hs), d).wait_recv()
    total = sums[0]
    for s in range(1, hs):
        total = total + sums[s]
    rms = jnp.sqrt(total[0:1] / full_width + EPS)
    inv_row = 1.0 / rms
    coef_row = total[4:5] / (full_width * (rms * rms * rms))
    for r in range(rows // tile):
        rs = slice(r * tile, (r + 1) * tile)
        inv = jnp.broadcast_to(inv_row[:, rs], (tile, tile)).T
        coef = jnp.broadcast_to(coef_row[:, rs], (tile, tile)).T

        def normed(h, carry):
            of = o_ref[rs, lanes(h)].astype(F32)
            sc = gain_ref[lanes(h)][None, :] * d_ref[rs, lanes(h)].astype(F32)
            d_ref[rs, lanes(h)] = (sc * inv - of * coef).astype(BF16)
            return carry

        lax.fori_loop(0, heads, normed, 0)

    loads[4].wait()
    own_terms(1, q_ref, d_ref)

    def local(c):
        row = lax.broadcasted_iota(jnp.int32, (GROUP, GROUP), 0)
        col = lax.broadcasted_iota(jnp.int32, (GROUP, GROUP), 1)
        for i in range(ch):
            h = c * ch + i
            for b in range(blocks):
                qb = q_ref[toks(b), lanes(h)]
                kb = k_ref[toks(b), lanes(h)]
                vb = v_ref[toks(b), lanes(h)]
                gb = d_ref[toks(b), lanes(h)]
                prods = jnp.where(row >= col, dot(gb, vb, 1, 1), 0.0).astype(BF16)
                acc_q[toks(b), lanes(h)] = dot(prods, kb, 1, 0)
                prods_t = jnp.where(col >= row, dot(vb, gb, 1, 1), 0.0).astype(BF16)
                acc_k[toks(b), lanes(h)] = dot(prods_t, qb, 1, 0)
                scores_t = jnp.where(col >= row, dot(kb, qb, 1, 1), 0.0).astype(BF16)
                acc_v[toks(b), lanes(h)] = dot(scores_t, gb, 1, 0)

    def finish(c):
        @pl.when(c >= raw)
        def _():
            for kind in range(2):
                for d in range(1, ys):
                    other = lax.rem(y + d, ys)

                    @pl.when(jnp.logical_not(later(kind, other)) | (hops[kind] > 0))
                    def _():
                        y_arrive(kind, c, d)

        for i in range(ch):
            h = c * ch + i
            ends = []
            for kind in range(2):
                total = zin[kind, h]
                for d in range(1, ys):
                    other = lax.rem(y + d, ys)
                    used = jnp.logical_not(later(kind, other)) | ((c >= raw) & (hops[kind] > 0))
                    total = total + jnp.where(used, slots[kind, other, h], 0.0)
                ends.append(total)
            fwd, bwd = [ends[0]], [ends[1]]
            for b in range(blocks - 1):
                fwd.append(fwd[-1] + terms[0, b, h])
                bwd.insert(0, bwd[0] + terms[1, blocks - 1 - b, h])
            for b in range(blocks):
                at = (toks(b), lanes(h))
                kb, vb, gb = k_ref[at], v_ref[at], d_ref[at]
                fs, bs = fwd[b].astype(BF16), bwd[b].astype(BF16)
                qg_out[at] = ((acc_q[at] + dot(gb, fs, 1, 1)) * factor).astype(BF16)
                kg_out[at] = ((acc_k[at] + dot(vb, bs, 1, 1)) * factor).astype(BF16)
                vg_out[at] = ((acc_v[at] + dot(kb, bs, 1, 0)) * factor).astype(BF16)

    last = jnp.maximum(start(0), start(1))
    edge = (hops[0] == 0) | (hops[1] == 0)

    def turn(t, carry):
        for kind in range(2):
            step(kind, t - start(kind), jnp.where(hops[kind] == 0, n - raw, 0))

        @pl.when(t - EARLY < n)
        def _():
            local(t - EARLY)

        place = t - last

        @pl.when((place >= n - raw) & (place < n))
        def _():
            finish(lax.rem(place + raw, n))

        settled = place - SETTLE

        @pl.when(edge & (settled >= 0) & (settled < n - raw))
        def _():
            finish(settled + raw)

        return carry

    lax.fori_loop(EARLY, steps + SETTLE, turn, 0)

    @pl.when(jnp.logical_not(edge))
    def _():
        lax.fori_loop(raw, n, lambda c, carry: (finish(c), carry)[1], 0)

    for d in range(1, hs):
        sum_copy(mine, d).wait_send()

    def sent(c, carry):
        for kind in range(2):
            for d in range(1, ys):
                other = lax.rem(y + d, ys)

                begun = jnp.where(c < raw, hops[kind] < zs - 1, hops[kind] > 0)

                @pl.when(later(kind, other) | begun)
                def _():
                    y_copy(kind, inc.at[kind], c, d).wait_send()

            @pl.when(hops[kind] < zs - 1)
            def _():
                z_copy(kind, c).wait_send()

        return carry

    lax.fori_loop(0, n, sent, 0)


def store_kernel(a, b, c, a_out, b_out, c_out, sem):
    part = a.shape[0] // STORES
    copies = []
    for i in range(STORES):
        at = slice(i * part, (i + 1) * part)
        for j, (src, dst) in enumerate(((a, a_out), (b, b_out), (c, c_out))):
            copies.append(pltpu.make_async_copy(src.at[at], dst.at[at], sem.at[j, i]))
    for copy in copies:
        copy.start()
    for copy in copies:
        copy.wait()


def shards(sizes, queries, keys, values, attn_out, out_grad, norm_gain):
    seqs, hs = sizes
    zs, ys = split_seq(seqs)
    rows, width = queries.shape
    heads = width // DH
    blocks = rows // GROUP
    ch = 1
    n = heads // ch
    raw = n // 3
    factor = 1.0 / math.sqrt(DH * rows * seqs)
    cfg = (zs, ys, hs, heads, ch, raw, rows, width * hs, factor)
    big = pltpu.VMEM((rows, width), BF16)
    acc = pltpu.VMEM((rows, width), F32)
    state = (heads, DH, DH)
    out = jax.ShapeDtypeStruct((rows, width), BF16)
    dma = pltpu.SemaphoreType.DMA
    flops = 2 * heads * blocks * (6 * GROUP * GROUP * DH + 5 * GROUP * DH * DH)
    held = pl.pallas_call(
        functools.partial(kernel, cfg),
        out_shape=(out, out, out),
        in_specs=[pl.BlockSpec(memory_space=pltpu.HBM)] * 6,
        out_specs=[pl.BlockSpec(memory_space=pltpu.VMEM)] * 3,
        scratch_shapes=[
            big, big, big, big, big,
            pltpu.VMEM((width,), F32),
            acc, acc, acc,
            pltpu.VMEM((2, blocks) + state, F32),
            pltpu.VMEM((2, ys) + state, F32),
            pltpu.VMEM((2,) + state, F32),
            pltpu.VMEM((2,) + state, F32),
            pltpu.VMEM((hs, 8, rows), F32),
            dma((6,)),
            dma((hs - 1,)),
            dma((hs,)),
            dma((2, ys - 1, n)),
            dma((2, ys, n)),
            dma((2, n)),
            dma((2, n)),
        ],
        cost_estimate=pl.CostEstimate(
            flops=flops, bytes_accessed=8 * rows * width * 2, transcendentals=0
        ),
        compiler_params=pltpu.CompilerParams(
            collective_id=0, has_side_effects=True, vmem_limit_bytes=42 * 1024 * 1024
        ),
    )(*[
        pltpu.with_memory_space_constraint(x, pltpu.HBM)
        for x in (queries, keys, values, attn_out, out_grad, norm_gain)
    ])
    return pl.pallas_call(
        store_kernel,
        out_shape=(out, out, out),
        in_specs=[pl.BlockSpec(memory_space=pl.ANY)] * 3,
        out_specs=[pl.BlockSpec(memory_space=pltpu.HBM)] * 3,
        scratch_shapes=[dma((3, STORES))],
        cost_estimate=pl.CostEstimate(
            flops=0, bytes_accessed=3 * rows * width * 2, transcendentals=0
        ),
        compiler_params=pltpu.CompilerParams(vmem_limit_bytes=4 * 1024 * 1024),
    )(*held)


def solution(mesh):
    sizes = (mesh.shape["seq"], mesh.shape["head"])
    spec = P("seq", "head")
    return jax.shard_map(
        functools.partial(shards, sizes),
        mesh=mesh,
        in_specs=(spec,) * 5 + (P("head"),),
        out_specs=(spec,) * 3,
        check_vma=False,
    )
```
